32 devices in a mesh: seq: 16 (over z, y, core), head: 2 (over x).
Axes of the slice: x: 2, y: 2, z: 4, core: 2. Of those that a mesh axis runs over, the one named last changes fastest.
Arguments:
- tokens: bfloat16 [2048, 2880], P('seq'), may hold values from -80 to 80
- gain: float32 [2880], replicated, may hold values from 0.1 to 1.9
- w_query: bfloat16 [2880, 1024], P('seq', 'head'), may hold values from -4 to 4
- w_key: bfloat16 [2880, 128], P('seq', 'head'), may hold values from -1 to 1
- w_value: bfloat16 [2880, 128], P('seq', 'head'), may hold values from -0.109375 to 0.109375
- w_out: bfloat16 [2880, 1024], P('seq', 'head'), may hold values from -0.1875 to 0.1875
- w_gate: float32 [2880], replicated, may hold values from -0.109375 to 0.109375
- steering: bfloat16 [16, 2880], replicated, may hold values from -5 to 5
- segment_ids: int32 [2048], P('seq'), may hold values from 0 to 7, never falling along the last dimension, each value on 1 to 512 neighbouring positions
- steer_index: int32 [2048], P('seq'), may hold values from 0 to 15
- grad_out: bfloat16 [2048, 2880], P('seq'), may hold values from -6 to 6
Outputs:
- layer_out: bfloat16 [2048, 2880], P('seq', 'head')
- grad_tokens: bfloat16 [2048, 2880], P('seq', 'head')
- steer_grad: float32 [16, 2880], P(None, 'head')
The draws below stay inside these ranges and needn't reach their ends.
Inputs may be any that keep to these rules, and one draw needn't show every extreme that they name: `segment_ids`: the ids never fall along the tokens; each id names one packed document of at most 512 tokens.
All inputs are finite; a program needn't handle non-finite values.
Results may differ from the reference program's by a relative error of at most 0.011.
Values may be sent and summed in bfloat16 or wider, within the bound.
A program may use at most 64 MiB of HBM per device.

```python
import math
import jax
import jax.numpy as jnp
import numpy as np
from jax import lax

D = 2880
HD = 64
QPK = 8
WIN = 128
NSTEER = 16
TOK_DEV = 128
KVH = 2
QH = 16
TOKENS = 2048
DOCS = 8
DOC_MAX = 512


def key_matrix(key):
    base = jax.random.truncated_normal(jax.random.fold_in(key, 11), -4.0, 4.0, (D, KVH * HD), jnp.float32)
    return base * D ** (-0.5)


def draw_w_key(key, part):
    return key_matrix(key).astype(jnp.bfloat16)


def draw_w_query(key, part):
    base = jax.random.truncated_normal(jax.random.fold_in(key, 12), -4.0, 4.0, (D, QH * HD), jnp.float32) * D ** (-0.5)
    return jnp.clip(base, -4.0, 4.0).astype(jnp.bfloat16)


def draw_tokens(key, part):
    row_scale = jnp.exp(jax.random.uniform(jax.random.fold_in(key, 21), (TOKENS, 1), jnp.float32, -1.15, 1.15))
    col_scale = jnp.exp(jax.random.uniform(jax.random.fold_in(key, 22), (1, D), jnp.float32, -1.15, 1.15))
    noise = jax.random.truncated_normal(jax.random.fold_in(key, 23), -4.0, 4.0, (TOKENS, D), jnp.float32)
    return (noise * row_scale * col_scale).astype(jnp.bfloat16)


def touch_ends(drawn, rng, smallest, high):
    place = [jax.random.randint(jax.random.fold_in(rng, axis), (), 0, length) for axis, length in enumerate(drawn.shape)]
    widest = drawn.shape.index(max(drawn.shape))
    neighbour = place[:widest] + [(place[widest] + 1) % drawn.shape[widest]] + place[widest + 1:]
    return drawn.at[tuple(place)].set(smallest).at[tuple(neighbour)].set(high)


def block_scale(rng, extent, shards, low, top_value):
    loudness = 1.0
    for axis_at, blocks in shards:
        draws = jax.random.uniform(jax.random.fold_in(jax.random.fold_in(rng, 6), axis_at), (blocks,), jnp.float32, low / len(shards), top_value / len(shards))
        loudness = loudness * jnp.repeat(jnp.exp(draws), extent[axis_at] // blocks).reshape((-1,) + (1,) * (len(extent) - 1 - axis_at))
    return loudness


def length_profile(amount, total, reach, skew):
    loads = [(1 << 20) // math.isqrt(standing ** skew) + 1 for standing in range(2, amount + 1)]
    spare, holding = total - reach - (amount - 1), [1] * (amount - 1)
    while spare > 0:
        movable = [i for i in range(amount - 1) if holding[i] < reach]
        whole, budget = sum([loads[i] for i in movable]), spare
        for i in movable:
            addition = min(reach - holding[i], max(1, budget * loads[i] // whole), spare)
            holding[i] = holding[i] + addition
            spare = spare - addition
    return np.array([reach] + holding)


def ragged(key, count, total, most, slope):
    if count == 2:
        one = jax.random.randint(key, (), max(1, total - most), min(most, total - 1) + 1)
        return jnp.stack([one, total - one])
    tallies = jnp.asarray(length_profile(count, total, most, slope), jnp.int32)
    couples = (count - 1) // 2
    source_of, taker = tallies[1:1 + 2 * couples:2], tallies[2:2 + 2 * couples:2]
    margin = jnp.minimum(source_of - 1, most - taker)
    passed = jax.random.randint(jax.random.fold_in(key, 1), (couples,), 0, 1 << 20) % (margin + 1)
    tallies = tallies.at[1:1 + 2 * couples:2].set(source_of - passed).at[2:2 + 2 * couples:2].set(taker + passed)
    return tallies[jax.random.permutation(jax.random.fold_in(key, 2), count)]


def scatter_about(rng, extent, spread, most, split=(), held_as=jnp.bfloat16):
    values = jax.random.normal(rng, extent, jnp.float32) * spread
    if len(split) > 0:
        values = block_scale(rng, extent, split, -0.22, 0.18) * values
    return jnp.clip(values, min=-most, max=most).astype(held_as)


def setup_inputs(seed: int = 0) -> dict:
    splits = jax.random.split(jax.random.key(seed), 12)
    tokens = draw_tokens(jax.random.fold_in(splits[11], 71), 0)
    gain = jnp.clip(1.0 + 0.18 * jax.random.normal(splits[1], (D,), jnp.float32), 0.1, 1.9)
    w_query = draw_w_query(jax.random.fold_in(splits[11], 71), 0)
    w_key = draw_w_key(jax.random.fold_in(splits[11], 71), 0)
    w_value = scatter_about(splits[4], (D, KVH * HD), D ** -0.5, 0.109375, ((0, 16), (1, 2)))
    w_out = scatter_about(splits[5], (D, QH * HD), (QH * HD) ** -0.5, 0.1875, ((0, 16), (1, 2)))
    w_gate = scatter_about(splits[6], (D,), D ** -0.5, 0.109375, (), jnp.float32)
    steering = scatter_about(splits[7], (NSTEER, D), 1.0, 5.0)
    segment_ids = jnp.searchsorted(jnp.cumsum(ragged(splits[8], DOCS, TOKENS, DOC_MAX, 2)), jnp.arange(TOKENS), side="right").astype(jnp.int32)
    steer_index = touch_ends(jax.random.randint(splits[9], (TOKENS,), 0, NSTEER), jax.random.fold_in(splits[9], 1), 0, NSTEER - 1).astype(jnp.int32)
    grad_out = scatter_about(splits[10], (TOKENS, D), 1.0, 6.0, ((0, 16),))
    return dict(tokens=tokens, gain=gain, w_query=w_query, w_key=w_key, w_value=w_value, w_out=w_out, w_gate=w_gate, steering=steering, segment_ids=segment_ids, steer_index=steer_index, grad_out=grad_out)


EPSILON = 1e-05
HIGHEST = lax.Precision.HIGHEST

def normalize(tokens, gain):
    tokens_f = tokens.astype(jnp.float32)
    inverse = lax.rsqrt(lax.optimization_barrier(jnp.mean(tokens_f * tokens_f, axis=-1, keepdims=True)) + EPSILON)
    unit_rows = tokens_f * inverse
    return (unit_rows, inverse, (unit_rows * gain).astype(jnp.bfloat16))

def rounded(values_f):
    return lax.optimization_barrier(values_f.astype(jnp.bfloat16)).astype(jnp.float32)

def contract(left, right):
    return lax.dot_general(left, right, (((1,), (1,)), ((), ())), preferred_element_type=jnp.float32)

def band_mask(query_seg, key_seg, offset):
    query_count = query_seg.shape[0]
    key_count = key_seg.shape[0]
    query_pos = lax.broadcasted_iota(jnp.int32, (query_count, key_count), 0)
    key_pos = lax.broadcasted_iota(jnp.int32, (query_count, key_count), 1) - offset
    distance = query_pos - key_pos
    return (distance >= 0) & (distance < WIN) & (query_seg[:, None] == key_seg[None, :])

def block_probs(query_block, key_block, mask):
    scores = jnp.einsum('rgqd,kgd->gqrk', query_block.astype(jnp.float32), key_block.astype(jnp.float32)) * HD ** (-0.5)
    scores = jnp.where(mask[None, None], scores, -jnp.inf)
    highest = lax.optimization_barrier(jnp.max(scores, axis=-1, keepdims=True))
    raised = jnp.exp(scores - highest)
    return raised / lax.optimization_barrier(jnp.sum(raised, axis=-1, keepdims=True))

def reference(tokens, gain, w_query, w_key, w_value, w_out, w_gate, steering, segment_ids, steer_index, grad_out):
    unit_rows, inverse, normed = normalize(tokens, gain)
    query_all = jnp.dot(normed, w_query, preferred_element_type=jnp.float32).astype(jnp.bfloat16)
    key_all = jnp.dot(normed, w_key, preferred_element_type=jnp.float32).astype(jnp.bfloat16)
    value_all = jnp.dot(normed, w_value, preferred_element_type=jnp.float32).astype(jnp.bfloat16)
    padded_keys = jnp.concatenate([jnp.zeros((WIN, KVH * HD), jnp.bfloat16), key_all], axis=0)
    padded_values = jnp.concatenate([jnp.zeros((WIN, KVH * HD), jnp.bfloat16), value_all], axis=0)
    segment_all = segment_ids.astype(jnp.int32)
    padded_seg = jnp.concatenate([jnp.full((WIN,), -1, jnp.int32), segment_all], axis=0)
    block_ids = jnp.arange(TOKENS // TOK_DEV, dtype=jnp.int32)

    def pieces(block_id):
        start = block_id * TOK_DEV
        query_block = lax.dynamic_slice_in_dim(query_all, start, TOK_DEV, 0).reshape(TOK_DEV, KVH, QPK, HD)
        key_block = lax.dynamic_slice_in_dim(padded_keys, start, WIN + TOK_DEV, 0).reshape(WIN + TOK_DEV, KVH, HD)
        value_block = lax.dynamic_slice_in_dim(padded_values, start, WIN + TOK_DEV, 0).reshape(WIN + TOK_DEV, KVH, HD)
        query_seg = lax.dynamic_slice_in_dim(segment_all, start, TOK_DEV, 0)
        key_seg = lax.dynamic_slice_in_dim(padded_seg, start, WIN + TOK_DEV, 0)
        probs = block_probs(query_block, key_block, band_mask(query_seg, key_seg, WIN))
        return (query_block, key_block, value_block, probs)

    def forward_block(block_id):
        query_block, key_block, value_block, probs = pieces(block_id)
        mixed = jnp.einsum('gqrk,kgd->rgqd', rounded(probs), value_block.astype(jnp.float32))
        return mixed.reshape(TOK_DEV, QH * HD).astype(jnp.bfloat16)
    mixed_all = lax.map(forward_block, block_ids).reshape(TOKENS, QH * HD)
    group_cols = QPK * HD
    attn_sum = jnp.zeros((TOKENS, D), jnp.float32)
    for group_index in range(KVH):
        col_start = group_index * group_cols
        attn_sum = attn_sum + rounded(contract(mixed_all[:, col_start:col_start + group_cols], w_out[:, col_start:col_start + group_cols]))
    tokens_f = tokens.astype(jnp.float32)
    gate_value = jax.nn.sigmoid(jnp.dot(normed.astype(jnp.float32), w_gate, precision=HIGHEST))
    one_hot = (steer_index[:, None] == jnp.arange(NSTEER, dtype=jnp.int32)[None, :]).astype(jnp.float32)
    steer_rows = jnp.dot(one_hot, steering.astype(jnp.float32), precision=HIGHEST)
    layer_out = (tokens_f + attn_sum + gate_value[:, None] * steer_rows).astype(jnp.bfloat16)
    grad_f = grad_out.astype(jnp.float32)
    steer_grad = jnp.dot(one_hot.T, gate_value[:, None] * grad_f, precision=HIGHEST)
    grad_logit = gate_value * (1.0 - gate_value) * lax.optimization_barrier(jnp.sum(grad_f * steer_rows, axis=-1))
    grad_mixed = jnp.dot(grad_out, w_out, preferred_element_type=jnp.float32).astype(jnp.bfloat16)

    def backward_block(block_id):
        query_block, key_block, value_block, probs = pieces(block_id)
        start = block_id * TOK_DEV
        grad_block = lax.dynamic_slice_in_dim(grad_mixed, start, TOK_DEV, 0).reshape(TOK_DEV, KVH, QPK, HD).astype(jnp.float32)
        grad_values = jnp.einsum('gqrk,rgqd->kgd', rounded(probs), grad_block)
        grad_prob = jnp.einsum('rgqd,kgd->gqrk', grad_block, value_block.astype(jnp.float32))
        delta = lax.optimization_barrier(jnp.sum(probs * grad_prob, axis=-1, keepdims=True))
        grad_scores = rounded(probs * (grad_prob - delta) * HD ** (-0.5))
        grad_query = jnp.einsum('gqrk,kgd->rgqd', grad_scores, key_block.astype(jnp.float32)).astype(jnp.bfloat16)
        grad_keys = jnp.einsum('gqrk,rgqd->kgd', grad_scores, query_block.astype(jnp.float32))
        return (grad_query.reshape(TOK_DEV, QH * HD), grad_keys.reshape(WIN + TOK_DEV, KVH * HD), grad_values.reshape(WIN + TOK_DEV, KVH * HD))
    query_parts, key_parts, value_parts = lax.map(backward_block, block_ids)
    grad_query_all = query_parts.reshape(TOKENS, QH * HD)

    def settle(parts):
        own_rows = parts[:, WIN:]
        own_rows = own_rows.at[:-1, TOK_DEV - WIN:].add(parts[1:, :WIN])
        return own_rows.reshape(TOKENS, KVH * HD).astype(jnp.bfloat16)
    grad_key_all = settle(key_parts)
    grad_value_all = settle(value_parts)
    grad_normed = jnp.zeros((TOKENS, D), jnp.float32)
    for group_index in range(KVH):
        col_start = group_index * group_cols
        key_start = group_index * HD
        group_terms = contract(grad_query_all[:, col_start:col_start + group_cols], w_query[:, col_start:col_start + group_cols])
        group_terms = group_terms + contract(grad_key_all[:, key_start:key_start + HD], w_key[:, key_start:key_start + HD])
        group_terms = group_terms + contract(grad_value_all[:, key_start:key_start + HD], w_value[:, key_start:key_start + HD])
        grad_normed = grad_normed + rounded(group_terms)
    grad_normed = grad_normed + grad_logit[:, None] * w_gate[None, :]
    scaled = grad_normed * gain
    row_mean = lax.optimization_barrier(jnp.sum(scaled * unit_rows, axis=-1, keepdims=True)) / D
    grad_tokens = (grad_f + inverse * (scaled - unit_rows * row_mean)).astype(jnp.bfloat16)
    return (layer_out, grad_tokens, steer_grad)
```

```python
import functools
import jax
import jax.numpy as jnp
from jax import lax
from jax.experimental import pallas as pl
from jax.experimental.pallas import tpu as pltpu
from jax.sharding import PartitionSpec as P

WIN = 128
EPSILON = 1e-05
HIGHEST = lax.Precision.HIGHEST
MESH = pl.DeviceIdType.MESH
ROWS_OF_CHIPS = 4
F32 = jnp.float32
BF16 = jnp.bfloat16


def dot(left, right):
    return jnp.dot(left, right, preferred_element_type=F32)


def dot_t(left, right):
    return lax.dot_general(left, right, (((1,), (1,)), ((), ())), preferred_element_type=F32)


def t_dot(left, right):
    return lax.dot_general(left, right, (((0,), (0,)), ((), ())), preferred_element_type=F32)


def kernel(
    S,
    H,
    tok_ref,
    gain_ref,
    wq_ref,
    wk_ref,
    wv_ref,
    wo_ref,
    wg_ref,
    steer_ref,
    seg_ref,
    sidx_ref,
    go_ref,
    lay_ref,
    gtok_ref,
    sgrad_ref,
    qbuf,
    obuf,
    tok_c,
    go_c,
    norm_c,
    gain_c,
    wg_c,
    steer_c,
    qacc,
    gmacc,
    kvall,
    segbuf,
    pbuf,
    abuf,
    arecv,
    gbuf,
    grecv,
    rbuf,
    rrecv,
    hgsend,
    hgrecv,
    sacc,
    srecv,
    qsend,
    qrecv,
    osend,
    orecv,
    segsem,
    kvsem,
    hgsem,
    asend,
    arsem,
    gsend,
    grsem,
    rsend,
    rrsem,
    ssend,
    srsem,
):
    T, D = tok_ref.shape
    rows, group_cols = wq_ref.shape
    hd = wk_ref.shape[1]
    heads = group_cols // hd
    scale = hd ** (-0.5)
    cps = S // H
    C = S // 2
    half = C // 2
    Y = C // ROWS_OF_CHIPS
    steps = sacc.shape[0] - 1
    steer_count = steer_ref.shape[0]

    me = lax.axis_index("seq")
    h = lax.axis_index("head")
    core = me % 2
    chip = me // 2
    z, y = chip // Y, chip % Y
    odd = z % 2
    inner = z * (Y - 1) + (1 - odd) * (y - 1) + odd * (Y - 1 - y)
    outer = ROWS_OF_CHIPS * (Y - 1) + (ROWS_OF_CHIPS - 1 - z)
    pos = jnp.where(y == 0, outer, inner)

    def at(place):
        p = place % C
        zi = p // (Y - 1)
        o = p % (Y - 1)
        yi = jnp.where(zi % 2 == 0, 1 + o, Y - 1 - o)
        last = p >= ROWS_OF_CHIPS * (Y - 1)
        zz = jnp.where(last, ROWS_OF_CHIPS - 1 - (p - ROWS_OF_CHIPS * (Y - 1)), zi)
        yy = jnp.where(last, 0, yi)
        return (zz * Y + yy) * 2 + core

    cw, ccw = at(pos + 1), at(pos + C - 1)
    other = 1 - 2 * core
    sib = me + other
    after, before = (me + 1) % S, (me + S - 1) % S
    pairs = []
    for k in range(steps):
        bit = (me // (1 << k)) % 2
        pairs.append(me + (1 - 2 * bit) * (1 << k))
    peers = [(h + d) % H for d in range(1, H)]

    barrier = pltpu.get_barrier_semaphore()
    for target in [cw, ccw, sib, after, before] + pairs:
        pl.semaphore_signal(barrier, inc=1, device_id=(target, h), device_id_type=MESH)
    for peer in peers:
        pl.semaphore_signal(barrier, inc=1, device_id=(me, peer), device_id_type=MESH)

    qbuf[me] = jnp.zeros(qbuf.shape[1:], BF16)
    obuf[me] = jnp.zeros(obuf.shape[1:], BF16)
    qbuf[me, :rows, :group_cols] = wq_ref[...]
    qbuf[me, :rows, group_cols:] = jnp.concatenate([wk_ref[...], wv_ref[...]], axis=1)
    obuf[me, :rows, :] = wo_ref[...]
    segbuf[1] = jnp.broadcast_to(seg_ref[...], segbuf.shape[1:])

    pl.semaphore_wait(barrier, 5 + steps + H - 1)

    def remote(src, dst, send, recv, seq, head):
        return pltpu.make_async_remote_copy(
            src_ref=src,
            dst_ref=dst,
            send_sem=send,
            recv_sem=recv,
            device_id=(seq, head),
            device_id_type=MESH,
        )

    targets = (cw, ccw, sib)

    def q_copy(slot, way):
        return remote(
            qbuf.at[slot], qbuf.at[slot], qsend.at[way, slot], qrecv.at[slot], targets[way], h
        )

    def o_copy(slot, way):
        return remote(
            obuf.at[slot], obuf.at[slot], osend.at[way, slot], orecv.at[slot], targets[way], h
        )

    for way in range(3):
        q_copy(me, way).start()
    seg_copy = remote(segbuf.at[1], segbuf.at[0], segsem.at[0], segsem.at[1], after, h)
    seg_copy.start()

    tokens = tok_ref[...].astype(F32)
    inverse = lax.rsqrt(jnp.sum(tokens * tokens, axis=1, keepdims=True) * (1.0 / D) + EPSILON)
    normed = (tokens * inverse * gain_ref[...]).astype(BF16)
    gate = jax.nn.sigmoid(jnp.sum(normed.astype(F32) * wg_ref[...], axis=1, keepdims=True))
    for ref in (tok_c, go_c, norm_c, gain_c, wg_c, steer_c):
        ref[...] = jnp.zeros(ref.shape, ref.dtype)
    for c in range(S):
        cols = slice(c * rows, (c + 1) * rows)
        tok_c[c, :, :rows] = tok_ref[:, cols]
        go_c[c, :, :rows] = go_ref[:, cols]
        norm_c[c, :, :rows] = normed[:, cols]
        gain_c[c, :, :rows] = gain_ref[:, cols]
        wg_c[c, :, :rows] = wg_ref[:, cols]
        steer_c[c, :, :rows] = steer_ref[:, cols]

    same = lax.broadcasted_iota(jnp.int32, (T, T), 0) == lax.broadcasted_iota(jnp.int32, (T, T), 1)

    def column(row):
        return jnp.sum(jnp.where(same, jnp.broadcast_to(row, (T, T)), 0), axis=1, keepdims=True)

    sidx_row = sidx_ref[...]
    sidx_col = column(sidx_row)
    one_hot = (lax.broadcasted_iota(jnp.int32, (T, steer_count), 1) == sidx_col).astype(F32)
    one_hot_b = one_hot.astype(BF16)
    one_hot_t = (lax.broadcasted_iota(jnp.int32, (steer_count, T), 0) == sidx_row).astype(F32)

    def logit_step(c, total):
        return total + go_c[c].astype(F32) * dot(one_hot_b, steer_c[c])

    logit_sum = lax.fori_loop(0, S, logit_step, jnp.zeros(go_c.shape[1:], F32))
    grad_logit = gate * (1.0 - gate) * jnp.sum(logit_sum, axis=1, keepdims=True)

    @pl.loop(0, cps)
    def _(j):
        sacc[0, j] = jnp.dot(
            one_hot_t,
            gate * go_c[h * cps + j].astype(F32),
            precision=HIGHEST,
            preferred_element_type=F32,
        )

    def s_copy(k):
        return remote(sacc.at[k], srecv.at[k], ssend.at[k], srsem.at[k], pairs[k], h)

    def s_finish(k):
        s_copy(k).wait_recv()
        sacc[k + 1] = sacc[k] + srecv[k]

    def q_acc(slot):
        qacc[...] += dot(norm_c[slot], qbuf[slot])

    qacc[...] = dot(norm_c[me], qbuf[me])

    def q_step(t, carry):
        a, b = at(pos + C - t), at(pos + t)
        q_copy(a, 0).wait_recv()
        q_copy(a, 0).start()
        q_copy(a, 2).start()
        q_copy(b, 1).wait_recv()

        @pl.when(t < half - 1)
        def _():
            q_copy(b, 1).start()

        q_copy(b, 2).start()
        q_acc(a)
        q_acc(b)
        return carry

    def q_sib(t, carry):
        a, b = at(pos + C - t) + other, at(pos + t) + other
        q_copy(a, 2).wait_recv()
        q_acc(a)
        q_copy(b, 2).wait_recv()
        q_acc(b)
        return carry

    q_copy(sib, 2).wait_recv()
    q_acc(sib)

    def q_both(t, carry):
        q_step(t, carry)
        return q_sib(t, carry)

    lax.fori_loop(1, half, q_both, 0)
    for way in range(3):
        o_copy(me, way).start()
    far = at(pos + half)
    q_copy(far, 0).wait_recv()
    q_copy(far, 2).start()
    q_acc(far)
    q_copy(far + other, 2).wait_recv()
    q_acc(far + other)

    qkv = qacc[...].astype(BF16)
    kvall[T:] = qkv[:, group_cols:]
    kv_copy = remote(kvall.at[pl.ds(T, T)], kvall.at[pl.ds(0, T)], kvsem.at[0], kvsem.at[1], after, h)
    kv_copy.start()

    def o_fwd(t):
        b, a = at(pos + t), at(pos + C - t)
        o_copy(b, 1).wait_recv()
        o_copy(b, 1).start()
        o_copy(b, 2).start()
        o_copy(a, 0).wait_recv()

        @pl.when(t < half - 1)
        def _():
            o_copy(a, 0).start()

        o_copy(a, 2).start()

    seg_copy.wait_recv()
    halo_seg = jnp.where(me > 0, segbuf[0, 0:1, :], -1)
    seg_row = seg_ref[...]
    query_seg = column(seg_row)
    key_seg = jnp.concatenate([halo_seg, seg_row], axis=1)
    distance = (
        lax.broadcasted_iota(jnp.int32, (T, 2 * T), 0)
        - lax.broadcasted_iota(jnp.int32, (T, 2 * T), 1)
        + T
    )
    mask = (distance >= 0) & (distance < WIN) & (query_seg == key_seg)

    kv_copy.wait_recv()
    keys = kvall[:, :hd]
    values = kvall[:, hd:]
    mixed_parts = []
    for i in range(heads):
        scores = dot_t(qkv[:, i * hd : (i + 1) * hd], keys) * scale
        scores = jnp.where(mask, scores, -1e30)
        raised = jnp.exp(scores - jnp.max(scores, axis=1, keepdims=True))
        probs = raised / jnp.sum(raised, axis=1, keepdims=True)
        pbuf[i] = probs
        mixed_parts.append(dot(probs.astype(BF16), values).astype(BF16))
        if i == heads // 2 - 1:
            o_fwd(1)
        if i == heads - 1:
            o_fwd(2)
    mixed = jnp.concatenate(mixed_parts, axis=1)

    def a_copy(slot):
        return remote(
            abuf.at[slot], arecv.at[h, slot % cps], asend.at[slot], arsem.at[h, slot % cps], me, slot // cps
        )

    def o_acc(slot):
        gmacc[...] += dot(go_c[slot], obuf[slot])
        abuf[slot] = dot_t(mixed, obuf[slot]).astype(BF16)

        @pl.when(slot // cps != h)
        def _():
            a_copy(slot).start()

    gmacc[...] = jnp.zeros(gmacc.shape, F32)
    o_acc(me)
    o_copy(sib, 2).wait_recv()
    o_acc(sib)

    def o_work(t):
        b, a = at(pos + t), at(pos + C - t)
        o_acc(b)
        o_acc(a)
        for slot in (b + other, a + other):
            o_copy(slot, 2).wait_recv()
            o_acc(slot)

    o_work(1)
    o_work(2)

    def o_both(t, carry):
        o_fwd(t)
        o_work(t)
        return carry

    lax.fori_loop(3, half, o_both, 0)
    o_copy(far, 1).wait_recv()
    o_copy(far, 2).start()
    s_copy(0).start()
    o_acc(far)
    o_copy(far + other, 2).wait_recv()
    o_acc(far + other)

    grad_mixed = gmacc[...].astype(BF16)
    grad_query = []
    grad_keys = jnp.zeros((2 * T, hd), F32)
    grad_values = jnp.zeros((2 * T, hd), F32)
    for i in range(heads):
        part = grad_mixed[:, i * hd : (i + 1) * hd]
        probs = pbuf[i]
        grad_prob = dot_t(part, values)
        delta = jnp.sum(probs * grad_prob, axis=1, keepdims=True)
        grad_scores = (probs * (grad_prob - delta) * scale).astype(BF16)
        grad_query.append(dot(grad_scores, keys).astype(BF16))
        grad_keys = grad_keys + t_dot(grad_scores, qkv[:, i * hd : (i + 1) * hd])
        grad_values = grad_values + t_dot(probs.astype(BF16), part)
    grad_kv = jnp.concatenate([grad_keys, grad_values], axis=1)
    hgsend[...] = grad_kv[:T].astype(BF16)
    hg_copy = remote(hgsend, hgrecv, hgsem.at[0], hgsem.at[1], before, h)
    hg_copy.start()
    s_finish(0)
    s_copy(1).start()

    for j in range(cps):
        c = h * cps + j
        total = abuf[c].astype(F32)
        for peer in peers:
            remote(abuf.at[c], arecv.at[peer, j], asend.at[c], arsem.at[peer, j], me, peer).wait_recv()
            total = total + arecv[peer, j].astype(F32)
        steer_rows = dot(one_hot_b, steer_c[c])
        out = tok_c[c].astype(F32) + total + gate * steer_rows
        lay_ref[:, j * rows : (j + 1) * rows] = out[:, :rows].astype(BF16)

    s_finish(1)
    s_copy(2).start()
    hg_copy.wait_recv()
    kv_back = (grad_kv[T:] + hgrecv[...].astype(F32)).astype(BF16)
    grad_all = jnp.concatenate(grad_query + [kv_back], axis=1)

    def g_copy(slot):
        return remote(
            gbuf.at[slot], grecv.at[h, slot % cps], gsend.at[slot], grsem.at[h, slot % cps], me, slot // cps
        )

    def g_step(i, total):
        c = ((h + 1) * cps + i) % S
        term = dot_t(grad_all, qbuf[c]).astype(BF16)
        gbuf[c] = term

        @pl.when(c // cps != h)
        def _():
            g_copy(c).start()

        return total + term.astype(F32) * gain_c[c] * tok_c[c].astype(F32)

    row_terms = lax.fori_loop(0, S, g_step, jnp.zeros(go_c.shape[1:], F32))
    row_own = jnp.sum(row_terms, axis=1, keepdims=True) * inverse
    as_row = jnp.sum(jnp.where(same, jnp.broadcast_to(row_own, (T, T)), 0.0), axis=0, keepdims=True)
    rbuf[...] = jnp.broadcast_to(as_row, rbuf.shape)

    def r_copy(d):
        return remote(rbuf, rrecv.at[h], rsend.at[d], rrsem.at[h], me, peers[d])

    for d in range(H - 1):
        r_copy(d).start()
    for k in range(2, steps):
        s_finish(k)
        if k + 1 < steps:
            s_copy(k + 1).start()

    def gate_step(c, total):
        return total + wg_c[c] * gain_c[c] * tok_c[c].astype(F32)

    gate_terms = lax.fori_loop(0, S, gate_step, jnp.zeros(go_c.shape[1:], F32))
    row_total = row_own + grad_logit * inverse * jnp.sum(gate_terms, axis=1, keepdims=True)
    for j in range(cps):
        sgrad_ref[:, j * rows : (j + 1) * rows] = sacc[steps, j][:, :rows]
    for peer in peers:
        remote(rbuf, rrecv.at[peer], rsend.at[0], rrsem.at[peer], me, peer).wait_recv()
        row_total = row_total + column(rrecv[peer, 0:1, :])
    row_mean = row_total * (1.0 / D)

    for j in range(cps):
        c = h * cps + j
        total = gbuf[c].astype(F32)
        for peer in peers:
            remote(gbuf.at[c], grecv.at[peer, j], gsend.at[c], grsem.at[peer, j], me, peer).wait_recv()
            total = total + grecv[peer, j].astype(F32)
        scaled = (total + grad_logit * wg_c[c]) * gain_c[c]
        unit = tok_c[c].astype(F32) * inverse
        out = go_c[c].astype(F32) + inverse * (scaled - unit * row_mean)
        gtok_ref[:, j * rows : (j + 1) * rows] = out[:, :rows].astype(BF16)

    seg_copy.wait_send()
    kv_copy.wait_send()
    hg_copy.wait_send()
    for k in range(steps):
        s_copy(k).wait_send()
    for d in range(H - 1):
        r_copy(d).wait_send()

    def sent(i, carry):
        c = ((h + 1) * cps + i) % S
        a_copy(c).wait_send()
        g_copy(c).wait_send()
        return carry

    lax.fori_loop(0, S - cps, sent, 0)
    for way in range(3):
        q_copy(me, way).wait_send()
        o_copy(me, way).wait_send()

    def ring_sent(t, carry):
        a, b = at(pos + C - t), at(pos + t)
        q_copy(a, 0).wait_send()
        o_copy(b, 1).wait_send()

        @pl.when(t < half - 1)
        def _():
            q_copy(b, 1).wait_send()
            o_copy(a, 0).wait_send()

        for slot in (a, b):
            q_copy(slot, 2).wait_send()
            o_copy(slot, 2).wait_send()
        return carry

    lax.fori_loop(1, half, ring_sent, 0)
    q_copy(far, 2).wait_send()
    o_copy(far, 2).wait_send()


def shards(
    S,
    H,
    tokens,
    gain,
    w_query,
    w_key,
    w_value,
    w_out,
    w_gate,
    steering,
    segment_ids,
    steer_index,
    grad_out,
):
    T, D = tokens.shape
    rows, group_cols = w_query.shape
    hd = w_key.shape[1]
    heads = group_cols // hd
    wide = group_cols + 2 * hd
    pad = -(-rows // 16) * 16
    cps = S // H
    steps = S.bit_length() - 1
    steer_count = steering.shape[0]
    share = D // H
    dma = pltpu.SemaphoreType.DMA
    vmem = pltpu.VMEM
    scratch = [
        vmem((S, pad, wide), BF16),
        vmem((S, pad, group_cols), BF16),
        vmem((S, T, pad), BF16),
        vmem((S, T, pad), BF16),
        vmem((S, T, pad), BF16),
        vmem((S, 1, pad), F32),
        vmem((S, 1, pad), F32),
        vmem((S, steer_count, pad), BF16),
        vmem((T, wide), F32),
        vmem((T, group_cols), F32),
        vmem((2 * T, 2 * hd), BF16),
        vmem((2, 8, T), jnp.int32),
        vmem((heads, T, 2 * T), F32),
        vmem((S, T, pad), BF16),
        vmem((H, cps, T, pad), BF16),
        vmem((S, T, pad), BF16),
        vmem((H, cps, T, pad), BF16),
        vmem((8, T), F32),
        vmem((H, 8, T), F32),
        vmem((T, 2 * hd), BF16),
        vmem((T, 2 * hd), BF16),
        vmem((steps + 1, cps, steer_count, pad), F32),
        vmem((steps, cps, steer_count, pad), F32),
        dma((3, S)),
        dma((S,)),
        dma((3, S)),
        dma((S,)),
        dma((2,)),
        dma((2,)),
        dma((2,)),
        dma((S,)),
        dma((H, cps)),
        dma((S,)),
        dma((H, cps)),
        dma((max(H - 1, 1),)),
        dma((H,)),
        dma((steps,)),
        dma((steps,)),
    ]
    return pl.pallas_call(
        functools.partial(kernel, S, H),
        out_shape=(
            jax.ShapeDtypeStruct((T, share), BF16),
            jax.ShapeDtypeStruct((T, share), BF16),
            jax.ShapeDtypeStruct((steer_count, share), F32),
        ),
        in_specs=[pl.BlockSpec(memory_space=pltpu.VMEM)] * 11,
        out_specs=[pl.BlockSpec(memory_space=pltpu.VMEM)] * 3,
        scratch_shapes=scratch,
        compiler_params=pltpu.CompilerParams(
            collective_id=0, has_side_effects=True, vmem_limit_bytes=50 * 1024 * 1024
        ),
    )(
        tokens,
        gain.reshape(1, D),
        w_query,
        w_key,
        w_value,
        w_out,
        w_gate.reshape(1, D),
        steering,
        segment_ids.reshape(1, T),
        steer_index.reshape(1, T),
        grad_out,
    )


def solution(mesh):
    placed = (
        P("seq", None),
        P(),
        P("seq", "head"),
        P("seq", "head"),
        P("seq", "head"),
        P("seq", "head"),
        P(),
        P(),
        P("seq"),
        P("seq"),
        P("seq", None),
    )
    return jax.shard_map(
        functools.partial(shards, mesh.shape["seq"], mesh.shape["head"]),
        mesh=mesh,
        in_specs=placed,
        out_specs=(P("seq", "head"), P("seq", "head"), P(None, "head")),
        check_vma=False,
    )
```

```python
import functools
import jax
import jax.numpy as jnp
from jax import lax
from jax.experimental import pallas as pl
from jax.experimental.pallas import tpu as pltpu
from jax.sharding import PartitionSpec as P

WIN = 128
EPSILON = 1e-05
HIGHEST = lax.Precision.HIGHEST
MESH = pl.DeviceIdType.MESH
PIECES = 3
ROWS_OF_CHIPS = 4
F32 = jnp.float32
BF16 = jnp.bfloat16


def dot(left, right):
    return jnp.dot(left, right, preferred_element_type=F32)


def dot_t(left, right):
    return lax.dot_general(left, right, (((1,), (1,)), ((), ())), preferred_element_type=F32)


def t_dot(left, right):
    return lax.dot_general(left, right, (((0,), (0,)), ((), ())), preferred_element_type=F32)


def kernel(
    S,
    H,
    tok_ref,
    vec_ref,
    wq_ref,
    wk_ref,
    wv_ref,
    wo_ref,
    steer_ref,
    seg_ref,
    sidx_ref,
    go_ref,
    lay_ref,
    gtok_ref,
    sgrad_ref,
    qbuf,
    obuf,
    tok_p,
    go_p,
    go_c,
    norm_c,
    vec_p,
    steer_p,
    qacc,
    gmacc,
    kvall,
    segbuf,
    pbuf,
    abuf,
    arecv,
    gbuf,
    grecv,
    rbuf,
    rrecv,
    hgsend,
    hgrecv,
    sacc,
    srecv,
    qsend,
    qrecv,
    osend,
    orecv,
    segsem,
    kvsem,
    hgsem,
    asend,
    arsem,
    gsend,
    grsem,
    rsend,
    rrsem,
    ssend,
    srsem,
):
    T, D = tok_ref.shape
    rows, group_cols = wq_ref.shape
    hd = wk_ref.shape[1]
    heads = group_cols // hd
    scale = hd ** (-0.5)
    share = S // H // 2
    C = S // 2
    half = C // 2
    Y = C // ROWS_OF_CHIPS
    steps = sacc.shape[0] - 1
    steer_count = steer_ref.shape[0]

    me = lax.axis_index("seq")
    h = lax.axis_index("head")
    core = me % 2
    chip = me // 2
    z, y = chip // Y, chip % Y
    odd = z % 2
    inner = z * (Y - 1) + (1 - odd) * (y - 1) + odd * (Y - 1 - y)
    outer = ROWS_OF_CHIPS * (Y - 1) + (ROWS_OF_CHIPS - 1 - z)
    pos = jnp.where(y == 0, outer, inner)

    def at(place):
        p = place % C
        zi = p // (Y - 1)
        o = p % (Y - 1)
        yi = jnp.where(zi % 2 == 0, 1 + o, Y - 1 - o)
        last = p >= ROWS_OF_CHIPS * (Y - 1)
        zz = jnp.where(last, ROWS_OF_CHIPS - 1 - (p - ROWS_OF_CHIPS * (Y - 1)), zi)
        yy = jnp.where(last, 0, yi)
        return (zz * Y + yy) * 2 + core

    cw, ccw = at(pos + 1), at(pos + C - 1)
    other = 1 - 2 * core
    sib = me + other
    after, before = (me + 1) % S, (me + S - 1) % S
    pairs = []
    for k in range(steps):
        bit = (me // (1 << k)) % 2
        pairs.append(me + (1 - 2 * bit) * (1 << k))
    peers = [(h + d) % H for d in range(1, H)]

    barrier = pltpu.get_barrier_semaphore()
    for target in [cw, ccw, sib, after, before] + pairs:
        pl.semaphore_signal(barrier, inc=1, device_id=(target, h), device_id_type=MESH)
    for peer in peers:
        pl.semaphore_signal(barrier, inc=1, device_id=(me, peer), device_id_type=MESH)

    qbuf[me] = jnp.zeros(qbuf.shape[1:], BF16)
    obuf[me] = jnp.zeros(obuf.shape[1:], BF16)
    qbuf[me, :rows, :group_cols] = wq_ref[...]
    qbuf[me, :rows, group_cols:] = jnp.concatenate([wk_ref[...], wv_ref[...]], axis=1)
    obuf[me, :rows, :] = wo_ref[...]
    segbuf[1] = jnp.broadcast_to(seg_ref[...], segbuf.shape[1:])

    pl.semaphore_wait(barrier, 5 + steps + H - 1)

    def remote(src, dst, send, recv, seq, head):
        return pltpu.make_async_remote_copy(
            src_ref=src,
            dst_ref=dst,
            send_sem=send,
            recv_sem=recv,
            device_id=(seq, head),
            device_id_type=MESH,
        )

    targets = (cw, ccw, sib)
    piece = qbuf.shape[1] // PIECES

    def q_copy(slot, way, i):
        part = pl.ds(i * piece, piece)
        return remote(
            qbuf.at[slot, part],
            qbuf.at[slot, part],
            qsend.at[way, slot, i],
            qrecv.at[slot, i],
            targets[way],
            h,
        )

    def o_copy(slot, way, i):
        part = pl.ds(i * piece, piece)
        return remote(
            obuf.at[slot, part],
            obuf.at[slot, part],
            osend.at[way, slot, i],
            orecv.at[slot, i],
            targets[way],
            h,
        )

    every = range(PIECES)
    for i in every:
        for way in range(3):
            q_copy(me, way, i).start()
    seg_copy = remote(segbuf.at[1], segbuf.at[0], segsem.at[0], segsem.at[1], after, h)
    seg_copy.start()

    def q_fwd(t):
        a, b = at(pos + C - t), at(pos + t)
        for i in every:
            q_copy(a, 0, i).wait_recv()
            q_copy(a, 0, i).start()
            q_copy(a, 2, i).start()
            q_copy(b, 1, i).wait_recv()

            @pl.when(t < half - 1)
            def _():
                q_copy(b, 1, i).start()

            q_copy(b, 2, i).start()

    def o_fwd(t):
        b, a = at(pos + t), at(pos + C - t)
        for i in every:
            o_copy(b, 1, i).wait_recv()
            o_copy(b, 1, i).start()
            o_copy(b, 2, i).start()
            o_copy(a, 0, i).wait_recv()

            @pl.when(t < half - 1)
            def _():
                o_copy(a, 0, i).start()

            o_copy(a, 2, i).start()

    tokens = tok_ref[...].astype(F32)
    inverse = lax.rsqrt(jnp.sum(tokens * tokens, axis=1, keepdims=True) * (1.0 / D) + EPSILON)
    normed = (tokens * inverse * vec_ref[0:1, :]).astype(BF16)
    norm_c[...] = jnp.zeros(norm_c.shape, BF16)
    for c in range(S):
        norm_c[c, :, :rows] = normed[:, c * rows : (c + 1) * rows]

    def q_acc(slot):
        qacc[...] += dot(norm_c[slot], qbuf[slot])

    def q_sib(slot):
        for i in every:
            q_copy(slot, 2, i).wait_recv()
        q_acc(slot)

    def q_work(t):
        a, b = at(pos + C - t), at(pos + t)
        q_acc(a)
        q_acc(b)
        q_sib(a + other)
        q_sib(b + other)

    q_fwd(1)
    qacc[...] = dot(norm_c[me], qbuf[me])
    q_sib(sib)
    gate = jax.nn.sigmoid(
        jnp.sum(normed.astype(F32) * vec_ref[1:2, :], axis=1, keepdims=True)
    )
    for ref in (tok_p, go_p, go_c, vec_p, steer_p):
        ref[...] = jnp.zeros(ref.shape, ref.dtype)
    for c in range(S // 2):
        cols = slice(c * 2 * rows, (c + 1) * 2 * rows)
        tok_p[c, :, : 2 * rows] = tok_ref[:, cols]
        go_p[c, :, : 2 * rows] = go_ref[:, cols]
        vec_p[c, :, : 2 * rows] = vec_ref[:, cols]
        steer_p[c, :, : 2 * rows] = steer_ref[:, cols]
    for c in range(S):
        go_c[c, :, :rows] = go_ref[:, c * rows : (c + 1) * rows]

    def q_both(t, carry):
        q_fwd(t)
        q_work(t - 1)
        return carry

    lax.fori_loop(2, half, q_both, 0)
    for i in every:
        for way in range(3):
            o_copy(me, way, i).start()
    q_work(half - 1)
    far = at(pos + half)
    for i in every:
        q_copy(far, 0, i).wait_recv()
        q_copy(far, 2, i).start()
    q_acc(far)
    q_sib(far + other)

    qkv = qacc[...].astype(BF16)
    kvall[T:] = qkv[:, group_cols:]
    kv_copy = remote(
        kvall.at[pl.ds(T, T)], kvall.at[pl.ds(0, T)], kvsem.at[0], kvsem.at[1], after, h
    )
    kv_copy.start()

    same = lax.broadcasted_iota(jnp.int32, (T, T), 0) == lax.broadcasted_iota(jnp.int32, (T, T), 1)

    def column(row):
        return jnp.sum(jnp.where(same, jnp.broadcast_to(row, (T, T)), 0), axis=1, keepdims=True)

    sidx_row = sidx_ref[...]
    sidx_col = column(sidx_row)
    one_hot_b = (
        (lax.broadcasted_iota(jnp.int32, (T, steer_count), 1) == sidx_col).astype(F32).astype(BF16)
    )
    one_hot_t = (lax.broadcasted_iota(jnp.int32, (steer_count, T), 0) == sidx_row).astype(F32)

    def logit_step(c, total):
        return total + go_p[c].astype(F32) * dot(one_hot_b, steer_p[c])

    logit_sum = lax.fori_loop(0, S // 2, logit_step, jnp.zeros(go_p.shape[1:], F32))
    grad_logit = gate * (1.0 - gate) * jnp.sum(logit_sum, axis=1, keepdims=True)

    @pl.loop(0, share)
    def _(j):
        sacc[0, j] = jnp.dot(
            one_hot_t,
            gate * go_p[h * share + j].astype(F32),
            precision=HIGHEST,
            preferred_element_type=F32,
        )

    def s_copy(k):
        return remote(sacc.at[k], srecv.at[k], ssend.at[k], srsem.at[k], pairs[k], h)

    def s_finish(k):
        s_copy(k).wait_recv()
        sacc[k + 1] = sacc[k] + srecv[k]

    seg_copy.wait_recv()
    halo_seg = jnp.where(me > 0, segbuf[0, 0:1, :], -1)
    seg_row = seg_ref[...]
    query_seg = column(seg_row)
    key_seg = jnp.concatenate([halo_seg, seg_row], axis=1)
    distance = (
        lax.broadcasted_iota(jnp.int32, (T, 2 * T), 0)
        - lax.broadcasted_iota(jnp.int32, (T, 2 * T), 1)
        + T
    )
    mask = (distance >= 0) & (distance < WIN) & (query_seg == key_seg)

    kv_copy.wait_recv()
    keys = kvall[:, :hd]
    values = kvall[:, hd:]
    mixed_parts = []
    for i in range(heads):
        scores = dot_t(qkv[:, i * hd : (i + 1) * hd], keys) * scale
        scores = jnp.where(mask, scores, -1e30)
        raised = jnp.exp(scores - jnp.max(scores, axis=1, keepdims=True))
        probs = raised / jnp.sum(raised, axis=1, keepdims=True)
        pbuf[i] = probs
        mixed_parts.append(dot(probs.astype(BF16), values).astype(BF16))
        if i == heads // 2 - 1:
            o_fwd(1)
        if i == heads - 1:
            o_fwd(2)
    mixed = jnp.concatenate(mixed_parts, axis=1)

    def joined(low, high):
        fill = jnp.zeros((T, abuf.shape[2] - 2 * rows), F32)
        return jnp.concatenate([low[:, :rows], high[:, :rows], fill], axis=1).astype(BF16)

    def a_copy(pair):
        return remote(
            abuf.at[pair],
            arecv.at[h, pair % share],
            asend.at[pair],
            arsem.at[h, pair % share],
            me,
            pair // share,
        )

    def o_acc(slot):
        for i in every:
            o_copy(slot + other, 2, i).wait_recv()
        pair = slot // 2
        low, high = obuf[2 * pair], obuf[2 * pair + 1]
        abuf[pair] = joined(dot_t(mixed, low), dot_t(mixed, high))

        @pl.when(pair // share != h)
        def _():
            a_copy(pair).start()

        gmacc[...] += dot(go_c[2 * pair], low) + dot(go_c[2 * pair + 1], high)

    def o_work(t):
        o_acc(at(pos + t))
        o_acc(at(pos + C - t))

    gmacc[...] = jnp.zeros(gmacc.shape, F32)
    o_acc(me)
    o_work(1)

    def o_both(t, carry):
        o_fwd(t)
        o_work(t - 1)
        return carry

    lax.fori_loop(3, half, o_both, 0)
    for i in every:
        o_copy(far, 1, i).wait_recv()
        o_copy(far, 2, i).start()
    s_copy(0).start()
    o_work(half - 1)
    o_acc(far)

    grad_mixed = gmacc[...].astype(BF16)
    grad_query = []
    grad_keys = jnp.zeros((2 * T, hd), F32)
    grad_values = jnp.zeros((2 * T, hd), F32)
    for i in range(heads):
        part = grad_mixed[:, i * hd : (i + 1) * hd]
        probs = pbuf[i]
        grad_prob = dot_t(part, values)
        delta = jnp.sum(probs * grad_prob, axis=1, keepdims=True)
        grad_scores = (probs * (grad_prob - delta) * scale).astype(BF16)
        grad_query.append(dot(grad_scores, keys).astype(BF16))
        grad_keys = grad_keys + t_dot(grad_scores, qkv[:, i * hd : (i + 1) * hd])
        grad_values = grad_values + t_dot(probs.astype(BF16), part)
    grad_kv = jnp.concatenate([grad_keys, grad_values], axis=1)
    hgsend[...] = grad_kv[:T].astype(BF16)
    hg_copy = remote(hgsend, hgrecv, hgsem.at[0], hgsem.at[1], before, h)
    hg_copy.start()
    s_finish(0)
    s_copy(1).start()

    for j in range(share):
        c = h * share + j
        total = abuf[c].astype(F32)
        for peer in peers:
            remote(
                abuf.at[c], arecv.at[peer, j], asend.at[c], arsem.at[peer, j], me, peer
            ).wait_recv()
            total = total + arecv[peer, j].astype(F32)
        steer_rows = dot(one_hot_b, steer_p[c])
        out = tok_p[c].astype(F32) + total + gate * steer_rows
        lay_ref[:, j * 2 * rows : (j + 1) * 2 * rows] = out[:, : 2 * rows].astype(BF16)

    s_finish(1)
    s_copy(2).start()
    hg_copy.wait_recv()
    kv_back = (grad_kv[T:] + hgrecv[...].astype(F32)).astype(BF16)
    grad_all = jnp.concatenate(grad_query + [kv_back], axis=1)

    def g_copy(pair):
        return remote(
            gbuf.at[pair],
            grecv.at[h, pair % share],
            gsend.at[pair],
            grsem.at[h, pair % share],
            me,
            pair // share,
        )

    def g_step(i, total):
        c = ((h + 1) * share + i) % (S // 2)
        term = joined(dot_t(grad_all, qbuf[2 * c]), dot_t(grad_all, qbuf[2 * c + 1]))
        gbuf[c] = term

        @pl.when(c // share != h)
        def _():
            g_copy(c).start()

        return total + term.astype(F32) * vec_p[c, 0:1] * tok_p[c].astype(F32)

    row_terms = lax.fori_loop(0, S // 2, g_step, jnp.zeros(go_p.shape[1:], F32))
    row_own = jnp.sum(row_terms, axis=1, keepdims=True) * inverse
    as_row = jnp.sum(jnp.where(same, jnp.broadcast_to(row_own, (T, T)), 0.0), axis=0, keepdims=True)
    rbuf[...] = jnp.broadcast_to(as_row, rbuf.shape)

    def r_copy(d):
        return remote(rbuf, rrecv.at[h], rsend.at[d], rrsem.at[h], me, peers[d])

    for d in range(H - 1):
        r_copy(d).start()
    for k in range(2, steps):
        s_finish(k)
        if k + 1 < steps:
            s_copy(k + 1).start()

    def gate_step(c, total):
        return total + vec_p[c, 1:2] * vec_p[c, 0:1] * tok_p[c].astype(F32)

    gate_terms = lax.fori_loop(0, S // 2, gate_step, jnp.zeros(go_p.shape[1:], F32))
    row_total = row_own + grad_logit * inverse * jnp.sum(gate_terms, axis=1, keepdims=True)
    for j in range(share):
        sgrad_ref[:, j * 2 * rows : (j + 1) * 2 * rows] = sacc[steps, j][:, : 2 * rows]
    for peer in peers:
        remote(rbuf, rrecv.at[peer], rsend.at[0], rrsem.at[peer], me, peer).wait_recv()
        row_total = row_total + column(rrecv[peer, 0:1, :])
    row_mean = row_total * (1.0 / D)

    for j in range(share):
        c = h * share + j
        total = gbuf[c].astype(F32)
        for peer in peers:
            remote(
                gbuf.at[c], grecv.at[peer, j], gsend.at[c], grsem.at[peer, j], me, peer
            ).wait_recv()
            total = total + grecv[peer, j].astype(F32)
        scaled = (total + grad_logit * vec_p[c, 1:2]) * vec_p[c, 0:1]
        unit = tok_p[c].astype(F32) * inverse
        out = go_p[c].astype(F32) + inverse * (scaled - unit * row_mean)
        gtok_ref[:, j * 2 * rows : (j + 1) * 2 * rows] = out[:, : 2 * rows].astype(BF16)

    seg_copy.wait_send()
    kv_copy.wait_send()
    hg_copy.wait_send()
    for k in range(steps):
        s_copy(k).wait_send()
    for d in range(H - 1):
        r_copy(d).wait_send()

    def sent(i, carry):
        c = ((h + 1) * share + i) % (S // 2)
        a_copy(c).wait_send()
        g_copy(c).wait_send()
        return carry

    lax.fori_loop(0, S // 2 - share, sent, 0)
    for i in every:
        for way in range(3):
            q_copy(me, way, i).wait_send()
            o_copy(me, way, i).wait_send()

    def ring_sent(t, carry):
        a, b = at(pos + C - t), at(pos + t)
        for i in every:
            q_copy(a, 0, i).wait_send()
            o_copy(b, 1, i).wait_send()

            @pl.when(t < half - 1)
            def _():
                q_copy(b, 1, i).wait_send()
                o_copy(a, 0, i).wait_send()

            for slot in (a, b):
                q_copy(slot, 2, i).wait_send()
                o_copy(slot, 2, i).wait_send()
        return carry

    lax.fori_loop(1, half, ring_sent, 0)
    for i in every:
        q_copy(far, 2, i).wait_send()
        o_copy(far, 2, i).wait_send()


def shards(
    S,
    H,
    tokens,
    gain,
    w_query,
    w_key,
    w_value,
    w_out,
    w_gate,
    steering,
    segment_ids,
    steer_index,
    grad_out,
):
    T, D = tokens.shape
    rows, group_cols = w_query.shape
    hd = w_key.shape[1]
    heads = group_cols // hd
    wide = group_cols + 2 * hd
    pad = -(-rows // (16 * PIECES)) * 16 * PIECES
    pairs = S // H // 2
    pair_wide = -(-2 * rows // 128) * 128
    steps = S.bit_length() - 1
    steer_count = steering.shape[0]
    dma = pltpu.SemaphoreType.DMA
    vmem = pltpu.VMEM
    scratch = [
        vmem((S, pad, wide), BF16),
        vmem((S, pad, group_cols), BF16),
        vmem((S // 2, T, pair_wide), BF16),
        vmem((S // 2, T, pair_wide), BF16),
        vmem((S, T, pad), BF16),
        vmem((S, T, pad), BF16),
        vmem((S // 2, 2, pair_wide), F32),
        vmem((S // 2, steer_count, pair_wide), BF16),
        vmem((T, wide), F32),
        vmem((T, group_cols), F32),
        vmem((2 * T, 2 * hd), BF16),
        vmem((2, 8, T), jnp.int32),
        vmem((heads, T, 2 * T), F32),
        vmem((S // 2, T, pair_wide), BF16),
        vmem((H, pairs, T, pair_wide), BF16),
        vmem((S // 2, T, pair_wide), BF16),
        vmem((H, pairs, T, pair_wide), BF16),
        vmem((8, T), F32),
        vmem((H, 8, T), F32),
        vmem((T, 2 * hd), BF16),
        vmem((T, 2 * hd), BF16),
        vmem((steps + 1, pairs, steer_count, pair_wide), F32),
        vmem((steps, pairs, steer_count, pair_wide), F32),
        dma((3, S, PIECES)),
        dma((S, PIECES)),
        dma((3, S, PIECES)),
        dma((S, PIECES)),
        dma((2,)),
        dma((2,)),
        dma((2,)),
        dma((S // 2,)),
        dma((H, pairs)),
        dma((S // 2,)),
        dma((H, pairs)),
        dma((max(H - 1, 1),)),
        dma((H,)),
        dma((steps,)),
        dma((steps,)),
    ]
    return pl.pallas_call(
        functools.partial(kernel, S, H),
        out_shape=(
            jax.ShapeDtypeStruct((T, D // H), BF16),
            jax.ShapeDtypeStruct((T, D // H), BF16),
            jax.ShapeDtypeStruct((steer_count, D // H), F32),
        ),
        in_specs=[pl.BlockSpec(memory_space=pltpu.VMEM)] * 10,
        out_specs=[pl.BlockSpec(memory_space=pltpu.VMEM)] * 3,
        scratch_shapes=scratch,
        compiler_params=pltpu.CompilerParams(
            collective_id=0, has_side_effects=True, vmem_limit_bytes=50 * 1024 * 1024
        ),
    )(
        tokens,
        jnp.stack([gain, w_gate]),
        w_query,
        w_key,
        w_value,
        w_out,
        steering,
        segment_ids.reshape(1, T),
        steer_index.reshape(1, T),
        grad_out,
    )


def solution(mesh):
    placed = (
        P("seq", None),
        P(),
        P("seq", "head"),
        P("seq", "head"),
        P("seq", "head"),
        P("seq", "head"),
        P(),
        P(),
        P("seq"),
        P("seq"),
        P("seq", None),
    )
    return jax.shard_map(
        functools.partial(shards, mesh.shape["seq"], mesh.shape["head"]),
        mesh=mesh,
        in_specs=placed,
        out_specs=(P("seq", "head"), P("seq", "head"), P(None, "head")),
        check_vma=False,
    )
```

```python
import functools
import jax
import jax.numpy as jnp
from jax import lax
from jax.experimental import pallas as pl
from jax.experimental.pallas import tpu as pltpu
from jax.sharding import PartitionSpec as P

WIN = 128
EPSILON = 1e-05
HIGHEST = lax.Precision.HIGHEST
MESH = pl.DeviceIdType.MESH
PIECES = 3
ROWS_OF_CHIPS = 4
F32 = jnp.float32
BF16 = jnp.bfloat16


def dot(left, right):
    return jnp.dot(left, right, preferred_element_type=F32)


def dot_t(left, right):
    return lax.dot_general(left, right, (((1,), (1,)), ((), ())), preferred_element_type=F32)


def t_dot(left, right):
    return lax.dot_general(left, right, (((0,), (0,)), ((), ())), preferred_element_type=F32)


def kernel(
    S,
    H,
    tok_ref,
    gain_ref,
    wg_ref,
    wq_ref,
    wk_ref,
    wv_ref,
    wo_ref,
    steer_ref,
    seg_ref,
    sidx_ref,
    go_ref,
    lay_ref,
    gtok_ref,
    sgrad_ref,
    qbuf,
    obuf,
    tok_t,
    go_t,
    kv_t,
    vec_t,
    tok_p,
    go_p,
    go_c,
    norm_c,
    vec_p,
    steer_p,
    qacc,
    gmacc,
    kvall,
    segbuf,
    pbuf,
    abuf,
    arecv,
    gbuf,
    grecv,
    rbuf,
    rrecv,
    hgsend,
    hgrecv,
    sacc,
    srecv,
    qsend,
    qrecv,
    osend,
    orecv,
    segsem,
    kvsem,
    hgsem,
    asend,
    arsem,
    gsend,
    grsem,
    rsend,
    rrsem,
    ssend,
    srsem,
    loadsem,
):
    D, T = tok_ref.shape
    rows, group_cols = wq_ref.shape
    hd = wk_ref.shape[0]
    heads = group_cols // hd
    scale = hd ** (-0.5)
    share = S // H // 2
    C = S // 2
    half = C // 2
    Y = C // ROWS_OF_CHIPS
    steps = sacc.shape[0] - 1
    steer_count = steer_ref.shape[0]

    me = lax.axis_index("seq")
    h = lax.axis_index("head")
    core = me % 2
    chip = me // 2
    z, y = chip // Y, chip % Y
    odd = z % 2
    inner = z * (Y - 1) + (1 - odd) * (y - 1) + odd * (Y - 1 - y)
    outer = ROWS_OF_CHIPS * (Y - 1) + (ROWS_OF_CHIPS - 1 - z)
    pos = jnp.where(y == 0, outer, inner)

    def at(place):
        p = place % C
        zi = p // (Y - 1)
        o = p % (Y - 1)
        yi = jnp.where(zi % 2 == 0, 1 + o, Y - 1 - o)
        last = p >= ROWS_OF_CHIPS * (Y - 1)
        zz = jnp.where(last, ROWS_OF_CHIPS - 1 - (p - ROWS_OF_CHIPS * (Y - 1)), zi)
        yy = jnp.where(last, 0, yi)
        return (zz * Y + yy) * 2 + core

    cw, ccw = at(pos + 1), at(pos + C - 1)
    other = 1 - 2 * core
    sib = me + other
    after, before = (me + 1) % S, (me + S - 1) % S
    pairs = []
    for k in range(steps):
        bit = (me // (1 << k)) % 2
        pairs.append(me + (1 - 2 * bit) * (1 << k))
    peers = [(h + d) % H for d in range(1, H)]

    tok_load = pltpu.make_async_copy(tok_ref, tok_t, loadsem.at[0])
    go_load = pltpu.make_async_copy(go_ref, go_t, loadsem.at[1])
    tok_load.start()
    go_load.start()

    barrier = pltpu.get_barrier_semaphore()
    for target in [cw, ccw, sib, after, before] + pairs:
        pl.semaphore_signal(barrier, inc=1, device_id=(target, h), device_id_type=MESH)
    for peer in peers:
        pl.semaphore_signal(barrier, inc=1, device_id=(me, peer), device_id_type=MESH)

    qbuf[me] = jnp.zeros(qbuf.shape[1:], BF16)
    obuf[me] = jnp.zeros(obuf.shape[1:], BF16)
    qbuf[me, :rows, :group_cols] = wq_ref[...]
    kv_t[...] = jnp.zeros(kv_t.shape, F32)
    kv_t[:hd, :rows] = wk_ref[...].astype(F32)
    kv_t[hd:, :rows] = wv_ref[...].astype(F32)
    qbuf[me, :rows, group_cols:] = kv_t[...].T[:rows].astype(BF16)
    obuf[me, :rows, :] = wo_ref[...]
    segbuf[1] = jnp.broadcast_to(seg_ref[...], segbuf.shape[1:])

    pl.semaphore_wait(barrier, 5 + steps + H - 1)

    def remote(src, dst, send, recv, seq, head):
        return pltpu.make_async_remote_copy(
            src_ref=src,
            dst_ref=dst,
            send_sem=send,
            recv_sem=recv,
            device_id=(seq, head),
            device_id_type=MESH,
        )

    targets = (cw, ccw, sib)
    piece = qbuf.shape[1] // PIECES

    def q_copy(slot, way, i):
        part = pl.ds(i * piece, piece)
        return remote(
            qbuf.at[slot, part],
            qbuf.at[slot, part],
            qsend.at[way, slot, i],
            qrecv.at[slot, i],
            targets[way],
            h,
        )

    def o_copy(slot, way, i):
        part = pl.ds(i * piece, piece)
        return remote(
            obuf.at[slot, part],
            obuf.at[slot, part],
            osend.at[way, slot, i],
            orecv.at[slot, i],
            targets[way],
            h,
        )

    every = range(PIECES)
    for i in every:
        for way in range(3):
            q_copy(me, way, i).start()
    seg_copy = remote(segbuf.at[1], segbuf.at[0], segsem.at[0], segsem.at[1], after, h)
    seg_copy.start()

    def q_fwd(t):
        a, b = at(pos + C - t), at(pos + t)
        for i in every:
            q_copy(a, 0, i).wait_recv()
            q_copy(a, 0, i).start()
            q_copy(a, 2, i).start()
            q_copy(b, 1, i).wait_recv()

            @pl.when(t < half - 1)
            def _():
                q_copy(b, 1, i).start()

            q_copy(b, 2, i).start()

    def o_fwd(t):
        b, a = at(pos + t), at(pos + C - t)
        for i in every:
            o_copy(b, 1, i).wait_recv()
            o_copy(b, 1, i).start()
            o_copy(b, 2, i).start()
            o_copy(a, 0, i).wait_recv()

            @pl.when(t < half - 1)
            def _():
                o_copy(a, 0, i).start()

            o_copy(a, 2, i).start()

    same = lax.broadcasted_iota(jnp.int32, (T, T), 0) == lax.broadcasted_iota(jnp.int32, (T, T), 1)

    def column(row):
        return jnp.sum(
            jnp.where(same, jnp.broadcast_to(row, (T, T)), 0), axis=1, keepdims=True
        )

    vec_t[0:1] = gain_ref[...].reshape(1, D)
    vec_t[1:2] = wg_ref[...].reshape(1, D)
    vec_p[...] = jnp.zeros(vec_p.shape, F32)
    steer_p[...] = jnp.zeros(steer_p.shape, BF16)
    for c in range(S // 2):
        cols = slice(c * 2 * rows, (c + 1) * 2 * rows)
        vec_p[c, :, : 2 * rows] = vec_t[:, cols]
        steer_p[c, :, : 2 * rows] = steer_ref[:, cols]
    gap = jnp.zeros((T, norm_c.shape[2] - rows), F32)

    def halves(value):
        low = jnp.concatenate([value[:, :rows], gap], axis=1)
        high = jnp.concatenate([value[:, rows : 2 * rows], gap], axis=1)
        return low.astype(BF16), high.astype(BF16)

    def pair_rows(value, c):
        fill = jnp.zeros((tok_p.shape[2] - 2 * rows, T), F32)
        return jnp.concatenate([value[c * 2 * rows : (c + 1) * 2 * rows], fill], axis=0).T

    tok_load.wait()
    tokens = tok_t[...].astype(F32)
    inverse = column(
        lax.rsqrt(jnp.sum(tokens * tokens, axis=0, keepdims=True) * (1.0 / D) + EPSILON)
    )
    gate_sum = jnp.zeros(tok_p.shape[1:], F32)
    for c in range(S // 2):
        part = pair_rows(tokens, c)
        tok_p[c] = part.astype(BF16)
        normed = (part * inverse * vec_p[c, 0:1]).astype(BF16).astype(F32)
        norm_c[2 * c], norm_c[2 * c + 1] = halves(normed)
        gate_sum = gate_sum + normed * vec_p[c, 1:2]
    gate = jax.nn.sigmoid(jnp.sum(gate_sum, axis=1, keepdims=True))

    def q_acc(slot):
        qacc[...] += dot(norm_c[slot], qbuf[slot])

    def q_sib(slot):
        for i in every:
            q_copy(slot, 2, i).wait_recv()
        q_acc(slot)

    def q_work(t):
        a, b = at(pos + C - t), at(pos + t)
        q_acc(a)
        q_acc(b)
        q_sib(a + other)
        q_sib(b + other)

    q_fwd(1)
    qacc[...] = dot(norm_c[me], qbuf[me])
    q_sib(sib)
    go_load.wait()
    grads = go_t[...].astype(F32)
    for c in range(S // 2):
        part = pair_rows(grads, c)
        go_p[c] = part.astype(BF16)
        go_c[2 * c], go_c[2 * c + 1] = halves(part)

    def q_both(t, carry):
        q_fwd(t)
        q_work(t - 1)
        return carry

    lax.fori_loop(2, half, q_both, 0)
    for i in every:
        for way in range(3):
            o_copy(me, way, i).start()
    q_work(half - 1)
    far = at(pos + half)
    for i in every:
        q_copy(far, 0, i).wait_recv()
        q_copy(far, 2, i).start()
    q_acc(far)
    q_sib(far + other)

    qkv = qacc[...].astype(BF16)
    kvall[T:] = qkv[:, group_cols:]
    kv_copy = remote(
        kvall.at[pl.ds(T, T)], kvall.at[pl.ds(0, T)], kvsem.at[0], kvsem.at[1], after, h
    )
    kv_copy.start()

    sidx_row = sidx_ref[...]
    sidx_col = column(sidx_row)
    one_hot_b = (
        (lax.broadcasted_iota(jnp.int32, (T, steer_count), 1) == sidx_col).astype(F32).astype(BF16)
    )
    one_hot_t = (lax.broadcasted_iota(jnp.int32, (steer_count, T), 0) == sidx_row).astype(F32)

    def logit_step(c, total):
        return total + go_p[c].astype(F32) * dot(one_hot_b, steer_p[c])

    logit_sum = lax.fori_loop(0, S // 2, logit_step, jnp.zeros(go_p.shape[1:], F32))
    grad_logit = gate * (1.0 - gate) * jnp.sum(logit_sum, axis=1, keepdims=True)

    @pl.loop(0, share)
    def _(j):
        sacc[0, j] = jnp.dot(
            one_hot_t,
            gate * go_p[h * share + j].astype(F32),
            precision=HIGHEST,
            preferred_element_type=F32,
        )

    def s_copy(k):
        return remote(sacc.at[k], srecv.at[k], ssend.at[k], srsem.at[k], pairs[k], h)

    def s_finish(k):
        s_copy(k).wait_recv()
        sacc[k + 1] = sacc[k] + srecv[k]

    s_copy(0).start()

    def gate_step(c, total):
        return total + vec_p[c, 1:2] * vec_p[c, 0:1] * tok_p[c].astype(F32)

    gate_terms = lax.fori_loop(0, S // 2, gate_step, jnp.zeros(go_p.shape[1:], F32))
    row_gate = grad_logit * inverse * jnp.sum(gate_terms, axis=1, keepdims=True)

    seg_copy.wait_recv()
    halo_seg = jnp.where(me > 0, segbuf[0, 0:1, :], -1)
    seg_row = seg_ref[...]
    query_seg = column(seg_row)
    key_seg = jnp.concatenate([halo_seg, seg_row], axis=1)
    distance = (
        lax.broadcasted_iota(jnp.int32, (T, 2 * T), 0)
        - lax.broadcasted_iota(jnp.int32, (T, 2 * T), 1)
        + T
    )
    mask = (distance >= 0) & (distance < WIN) & (query_seg == key_seg)

    kv_copy.wait_recv()
    keys = kvall[:, :hd]
    values = kvall[:, hd:]
    mixed_parts = []
    for i in range(heads):
        scores = dot_t(qkv[:, i * hd : (i + 1) * hd], keys) * scale
        scores = jnp.where(mask, scores, -1e30)
        raised = jnp.exp(scores - jnp.max(scores, axis=1, keepdims=True))
        probs = raised / jnp.sum(raised, axis=1, keepdims=True)
        pbuf[i] = probs
        mixed_parts.append(dot(probs.astype(BF16), values).astype(BF16))
        if i == heads // 2 - 1:
            o_fwd(1)
        if i == heads - 1:
            o_fwd(2)
    mixed = jnp.concatenate(mixed_parts, axis=1)

    def joined(low, high):
        fill = jnp.zeros((T, abuf.shape[2] - 2 * rows), F32)
        return jnp.concatenate([low[:, :rows], high[:, :rows], fill], axis=1).astype(BF16)

    def a_copy(pair):
        return remote(
            abuf.at[pair],
            arecv.at[h, pair % share],
            asend.at[pair],
            arsem.at[h, pair % share],
            me,
            pair // share,
        )

    def o_acc(slot):
        for i in every:
            o_copy(slot + other, 2, i).wait_recv()
        pair = slot // 2
        low, high = obuf[2 * pair], obuf[2 * pair + 1]
        abuf[pair] = joined(dot_t(mixed, low), dot_t(mixed, high))

        @pl.when(pair // share != h)
        def _():
            a_copy(pair).start()

        gmacc[...] += dot(go_c[2 * pair], low) + dot(go_c[2 * pair + 1], high)

    def o_work(t):
        o_acc(at(pos + t))
        o_acc(at(pos + C - t))

    gmacc[...] = jnp.zeros(gmacc.shape, F32)
    o_acc(me)
    o_work(1)

    def o_both(t, carry):
        o_fwd(t)
        o_work(t - 1)
        return carry

    lax.fori_loop(3, half, o_both, 0)
    for i in every:
        o_copy(far, 1, i).wait_recv()
        o_copy(far, 2, i).start()
    s_finish(0)
    s_copy(1).start()
    o_work(half - 1)
    o_acc(far)

    grad_mixed = gmacc[...].astype(BF16)
    grad_query = []
    grad_keys = jnp.zeros((2 * T, hd), F32)
    grad_values = jnp.zeros((2 * T, hd), F32)
    for i in range(heads):
        part = grad_mixed[:, i * hd : (i + 1) * hd]
        probs = pbuf[i]
        grad_prob = dot_t(part, values)
        delta = jnp.sum(probs * grad_prob, axis=1, keepdims=True)
        grad_scores = (probs * (grad_prob - delta) * scale).astype(BF16)
        grad_query.append(dot(grad_scores, keys).astype(BF16))
        grad_keys = grad_keys + t_dot(grad_scores, qkv[:, i * hd : (i + 1) * hd])
        grad_values = grad_values + t_dot(probs.astype(BF16), part)
    grad_kv = jnp.concatenate([grad_keys, grad_values], axis=1)
    hgsend[...] = grad_kv[:T].astype(BF16)
    hg_copy = remote(hgsend, hgrecv, hgsem.at[0], hgsem.at[1], before, h)
    hg_copy.start()
    s_finish(1)
    s_copy(2).start()

    for j in range(share):
        c = h * share + j
        total = abuf[c].astype(F32)
        for peer in peers:
            remote(
                abuf.at[c], arecv.at[peer, j], asend.at[c], arsem.at[peer, j], me, peer
            ).wait_recv()
            total = total + arecv[peer, j].astype(F32)
        steer_rows = dot(one_hot_b, steer_p[c])
        out = tok_p[c].astype(F32) + total + gate * steer_rows
        lay_ref[:, j * 2 * rows : (j + 1) * 2 * rows] = out[:, : 2 * rows].astype(BF16)

    s_finish(2)
    s_copy(3).start()
    hg_copy.wait_recv()
    kv_back = (grad_kv[T:] + hgrecv[...].astype(F32)).astype(BF16)
    grad_all = jnp.concatenate(grad_query + [kv_back], axis=1)

    def g_copy(pair):
        return remote(
            gbuf.at[pair],
            grecv.at[h, pair % share],
            gsend.at[pair],
            grsem.at[h, pair % share],
            me,
            pair // share,
        )

    def g_step(i, total):
        c = ((h + 1) * share + i) % (S // 2)
        term = joined(dot_t(grad_all, qbuf[2 * c]), dot_t(grad_all, qbuf[2 * c + 1]))
        gbuf[c] = term

        @pl.when(c // share != h)
        def _():
            g_copy(c).start()

        return total + term.astype(F32) * vec_p[c, 0:1] * tok_p[c].astype(F32)

    row_terms = lax.fori_loop(0, S // 2, g_step, jnp.zeros(go_p.shape[1:], F32))
    row_own = jnp.sum(row_terms, axis=1, keepdims=True) * inverse
    as_row = jnp.sum(jnp.where(same, jnp.broadcast_to(row_own, (T, T)), 0.0), axis=0, keepdims=True)
    rbuf[...] = jnp.broadcast_to(as_row, rbuf.shape)

    def r_copy(d):
        return remote(rbuf, rrecv.at[h], rsend.at[d], rrsem.at[h], me, peers[d])

    for d in range(H - 1):
        r_copy(d).start()
    for k in range(3, steps):
        s_finish(k)
        if k + 1 < steps:
            s_copy(k + 1).start()

    row_total = row_own + row_gate
    for j in range(share):
        sgrad_ref[:, j * 2 * rows : (j + 1) * 2 * rows] = sacc[steps, j][:, : 2 * rows]
    for peer in peers:
        remote(rbuf, rrecv.at[peer], rsend.at[0], rrsem.at[peer], me, peer).wait_recv()
        row_total = row_total + column(rrecv[peer, 0:1, :])
    row_mean = row_total * (1.0 / D)

    for j in range(share):
        c = h * share + j
        total = gbuf[c].astype(F32)
        for peer in peers:
            remote(
                gbuf.at[c], grecv.at[peer, j], gsend.at[c], grsem.at[peer, j], me, peer
            ).wait_recv()
            total = total + grecv[peer, j].astype(F32)
        scaled = (total + grad_logit * vec_p[c, 1:2]) * vec_p[c, 0:1]
        unit = tok_p[c].astype(F32) * inverse
        out = go_p[c].astype(F32) + inverse * (scaled - unit * row_mean)
        gtok_ref[:, j * 2 * rows : (j + 1) * 2 * rows] = out[:, : 2 * rows].astype(BF16)

    seg_copy.wait_send()
    kv_copy.wait_send()
    hg_copy.wait_send()
    for k in range(steps):
        s_copy(k).wait_send()
    for d in range(H - 1):
        r_copy(d).wait_send()

    def sent(i, carry):
        c = ((h + 1) * share + i) % (S // 2)
        a_copy(c).wait_send()
        g_copy(c).wait_send()
        return carry

    lax.fori_loop(0, S // 2 - share, sent, 0)
    for i in every:
        for way in range(3):
            q_copy(me, way, i).wait_send()
            o_copy(me, way, i).wait_send()

    def ring_sent(t, carry):
        a, b = at(pos + C - t), at(pos + t)
        for i in every:
            q_copy(a, 0, i).wait_send()
            o_copy(b, 1, i).wait_send()

            @pl.when(t < half - 1)
            def _():
                q_copy(b, 1, i).wait_send()
                o_copy(a, 0, i).wait_send()

            for slot in (a, b):
                q_copy(slot, 2, i).wait_send()
                o_copy(slot, 2, i).wait_send()
        return carry

    lax.fori_loop(1, half, ring_sent, 0)
    for i in every:
        q_copy(far, 2, i).wait_send()
        o_copy(far, 2, i).wait_send()


def shards(
    S,
    H,
    tokens,
    gain,
    w_query,
    w_key,
    w_value,
    w_out,
    w_gate,
    steering,
    segment_ids,
    steer_index,
    grad_out,
):
    T, D = tokens.shape
    rows, group_cols = w_query.shape
    hd = w_key.shape[1]
    heads = group_cols // hd
    wide = group_cols + 2 * hd
    pad = -(-rows // (16 * PIECES)) * 16 * PIECES
    pairs = S // H // 2
    pair_wide = -(-2 * rows // 128) * 128
    steps = S.bit_length() - 1
    steer_count = steering.shape[0]
    dma = pltpu.SemaphoreType.DMA
    vmem = pltpu.VMEM
    scratch = [
        vmem((S, pad, wide), BF16),
        vmem((S, pad, group_cols), BF16),
        vmem((D, T), BF16),
        vmem((D, T), BF16),
        vmem((2 * hd, -(-rows // 128) * 128), F32),
        vmem((2, D), F32),
        vmem((S // 2, T, pair_wide), BF16),
        vmem((S // 2, T, pair_wide), BF16),
        vmem((S, T, pad), BF16),
        vmem((S, T, pad), BF16),
        vmem((S // 2, 2, pair_wide), F32),
        vmem((S // 2, steer_count, pair_wide), BF16),
        vmem((T, wide), F32),
        vmem((T, group_cols), F32),
        vmem((2 * T, 2 * hd), BF16),
        vmem((2, 8, T), jnp.int32),
        vmem((heads, T, 2 * T), F32),
        vmem((S // 2, T, pair_wide), BF16),
        vmem((H, pairs, T, pair_wide), BF16),
        vmem((S // 2, T, pair_wide), BF16),
        vmem((H, pairs, T, pair_wide), BF16),
        vmem((8, T), F32),
        vmem((H, 8, T), F32),
        vmem((T, 2 * hd), BF16),
        vmem((T, 2 * hd), BF16),
        vmem((steps + 1, pairs, steer_count, pair_wide), F32),
        vmem((steps, pairs, steer_count, pair_wide), F32),
        dma((3, S, PIECES)),
        dma((S, PIECES)),
        dma((3, S, PIECES)),
        dma((S, PIECES)),
        dma((2,)),
        dma((2,)),
        dma((2,)),
        dma((S // 2,)),
        dma((H, pairs)),
        dma((S // 2,)),
        dma((H, pairs)),
        dma((max(H - 1, 1),)),
        dma((H,)),
        dma((steps,)),
        dma((steps,)),
        dma((2,)),
    ]
    on_chip = pl.BlockSpec(memory_space=pltpu.VMEM)
    far_off = pl.BlockSpec(memory_space=pl.ANY)
    return pl.pallas_call(
        functools.partial(kernel, S, H),
        out_shape=(
            jax.ShapeDtypeStruct((T, D // H), BF16),
            jax.ShapeDtypeStruct((T, D // H), BF16),
            jax.ShapeDtypeStruct((steer_count, D // H), F32),
        ),
        in_specs=[far_off] + [on_chip] * 9 + [far_off],
        out_specs=[pl.BlockSpec(memory_space=pltpu.VMEM)] * 3,
        scratch_shapes=scratch,
        compiler_params=pltpu.CompilerParams(
            collective_id=0, has_side_effects=True, vmem_limit_bytes=50 * 1024 * 1024
        ),
    )(
        tokens.T,
        gain,
        w_gate,
        w_query,
        w_key.T,
        w_value.T,
        w_out,
        steering,
        segment_ids.reshape(1, T),
        steer_index.reshape(1, T),
        grad_out.T,
    )


def solution(mesh):
    placed = (
        P("seq", None),
        P(),
        P("seq", "head"),
        P("seq", "head"),
        P("seq", "head"),
        P("seq", "head"),
        P(),
        P(),
        P("seq"),
        P("seq"),
        P("seq", None),
    )
    return jax.shard_map(
        functools.partial(shards, mesh.shape["seq"], mesh.shape["head"]),
        mesh=mesh,
        in_specs=placed,
        out_specs=(P("seq", "head"), P("seq", "head"), P(None, "head")),
        check_vma=False,
    )
```

```python
import functools
import jax
import jax.numpy as jnp
from jax import lax
from jax.experimental import pallas as pl
from jax.experimental.pallas import tpu as pltpu
from jax.sharding import PartitionSpec as P

WIN = 128
EPSILON = 1e-05
HIGHEST = lax.Precision.HIGHEST
MESH = pl.DeviceIdType.MESH
PIECES = 3
ROWS_OF_CHIPS = 4
F32 = jnp.float32
BF16 = jnp.bfloat16


def dot(left, right):
    return jnp.dot(left, right, preferred_element_type=F32)


def dot_t(left, right):
    return lax.dot_general(left, right, (((1,), (1,)), ((), ())), preferred_element_type=F32)


def t_dot(left, right):
    return lax.dot_general(left, right, (((0,), (0,)), ((), ())), preferred_element_type=F32)


def kernel(
    S,
    H,
    tok_any,
    gain_any,
    wg_any,
    wq_any,
    wk_any,
    wv_any,
    wo_any,
    steer_any,
    seg_any,
    sidx_any,
    go_any,
    lay_ref,
    gtok_ref,
    sgrad_ref,
    qbuf,
    obuf,
    tok_t,
    gain_ref,
    wg_ref,
    wq_ref,
    wk_ref,
    wv_ref,
    wo_ref,
    steer_ref,
    seg_ref,
    sidx_ref,
    go_t,
    kv_t,
    vec_t,
    tok_p,
    go_p,
    go_c,
    norm_c,
    vec_p,
    steer_p,
    qacc,
    gmacc,
    kvall,
    segbuf,
    pbuf,
    abuf,
    arecv,
    gbuf,
    grecv,
    rbuf,
    rrecv,
    hgsend,
    hgrecv,
    sacc,
    srecv,
    qsend,
    qrecv,
    osend,
    orecv,
    segsem,
    kvsem,
    hgsem,
    asend,
    arsem,
    gsend,
    grsem,
    rsend,
    rrsem,
    ssend,
    srsem,
    loadsem,
):
    D, T = tok_any.shape
    rows, group_cols = wq_ref.shape
    hd = wk_ref.shape[0]
    heads = group_cols // hd
    scale = hd ** (-0.5)
    share = S // H // 2
    C = S // 2
    half = C // 2
    Y = C // ROWS_OF_CHIPS
    steps = sacc.shape[0] - 1
    steer_count = steer_ref.shape[0]

    me = lax.axis_index("seq")
    h = lax.axis_index("head")
    core = me % 2
    chip = me // 2
    z, y = chip // Y, chip % Y
    odd = z % 2
    inner = z * (Y - 1) + (1 - odd) * (y - 1) + odd * (Y - 1 - y)
    outer = ROWS_OF_CHIPS * (Y - 1) + (ROWS_OF_CHIPS - 1 - z)
    pos = jnp.where(y == 0, outer, inner)

    def at(place):
        p = place % C
        zi = p // (Y - 1)
        o = p % (Y - 1)
        yi = jnp.where(zi % 2 == 0, 1 + o, Y - 1 - o)
        last = p >= ROWS_OF_CHIPS * (Y - 1)
        zz = jnp.where(last, ROWS_OF_CHIPS - 1 - (p - ROWS_OF_CHIPS * (Y - 1)), zi)
        yy = jnp.where(last, 0, yi)
        return (zz * Y + yy) * 2 + core

    cw, ccw = at(pos + 1), at(pos + C - 1)
    other = 1 - 2 * core
    sib = me + other
    after, before = (me + 1) % S, (me + S - 1) % S
    pairs = []
    for k in range(steps):
        bit = (me // (1 << k)) % 2
        pairs.append(me + (1 - 2 * bit) * (1 << k))
    peers = [(h + d) % H for d in range(1, H)]

    loads = {}
    for i, (name, src, dst) in enumerate(
        [
            ("wq", wq_any, wq_ref),
            ("wk", wk_any, wk_ref),
            ("wv", wv_any, wv_ref),
            ("wo", wo_any, wo_ref),
            ("seg", seg_any, seg_ref),
            ("tok", tok_any, tok_t),
            ("gain", gain_any, gain_ref),
            ("wg", wg_any, wg_ref),
            ("steer", steer_any, steer_ref),
            ("sidx", sidx_any, sidx_ref),
            ("go", go_any, go_t),
        ]
    ):
        loads[name] = pltpu.make_async_copy(src, dst, loadsem.at[i])
        loads[name].start()

    barrier = pltpu.get_barrier_semaphore()
    for target in [cw, ccw, sib, after, before] + pairs:
        pl.semaphore_signal(barrier, inc=1, device_id=(target, h), device_id_type=MESH)
    for peer in peers:
        pl.semaphore_signal(barrier, inc=1, device_id=(me, peer), device_id_type=MESH)

    qbuf[me] = jnp.zeros(qbuf.shape[1:], BF16)
    obuf[me] = jnp.zeros(obuf.shape[1:], BF16)
    kv_t[...] = jnp.zeros(kv_t.shape, F32)
    for name in ("wq", "wk", "wv", "wo", "seg"):
        loads[name].wait()
    qbuf[me, :rows, :group_cols] = wq_ref[...]
    kv_t[:hd, :rows] = wk_ref[...].astype(F32)
    kv_t[hd:, :rows] = wv_ref[...].astype(F32)
    qbuf[me, :rows, group_cols:] = kv_t[...].T[:rows].astype(BF16)
    obuf[me, :rows, :] = wo_ref[...]
    segbuf[1] = jnp.broadcast_to(seg_ref[...], segbuf.shape[1:])

    pl.semaphore_wait(barrier, 5 + steps + H - 1)

    def remote(src, dst, send, recv, seq, head):
        return pltpu.make_async_remote_copy(
            src_ref=src,
            dst_ref=dst,
            send_sem=send,
            recv_sem=recv,
            device_id=(seq, head),
            device_id_type=MESH,
        )

    targets = (cw, ccw, sib)
    piece = qbuf.shape[1] // PIECES

    def q_copy(slot, way, i):
        part = pl.ds(i * piece, piece)
        return remote(
            qbuf.at[slot, part],
            qbuf.at[slot, part],
            qsend.at[way, slot, i],
            qrecv.at[slot, i],
            targets[way],
            h,
        )

    def o_copy(slot, way, i):
        part = pl.ds(i * piece, piece)
        return remote(
            obuf.at[slot, part],
            obuf.at[slot, part],
            osend.at[way, slot, i],
            orecv.at[slot, i],
            targets[way],
            h,
        )

    every = range(PIECES)
    for i in every:
        for way in range(3):
            q_copy(me, way, i).start()
    seg_copy = remote(segbuf.at[1], segbuf.at[0], segsem.at[0], segsem.at[1], after, h)
    seg_copy.start()

    def q_fwd(t):
        a, b = at(pos + C - t), at(pos + t)
        for i in every:
            q_copy(a, 0, i).wait_recv()
            q_copy(a, 0, i).start()
            q_copy(a, 2, i).start()
            q_copy(b, 1, i).wait_recv()

            @pl.when(t < half - 1)
            def _():
                q_copy(b, 1, i).start()

            q_copy(b, 2, i).start()

    def o_fwd(t):
        b, a = at(pos + t), at(pos + C - t)
        for i in every:
            o_copy(b, 1, i).wait_recv()
            o_copy(b, 1, i).start()
            o_copy(b, 2, i).start()
            o_copy(a, 0, i).wait_recv()

            @pl.when(t < half - 1)
            def _():
                o_copy(a, 0, i).start()

            o_copy(a, 2, i).start()

    same = lax.broadcasted_iota(jnp.int32, (T, T), 0) == lax.broadcasted_iota(jnp.int32, (T, T), 1)

    def column(row):
        return jnp.sum(
            jnp.where(same, jnp.broadcast_to(row, (T, T)), 0), axis=1, keepdims=True
        )

    for name in ("gain", "wg", "steer", "sidx"):
        loads[name].wait()
    vec_t[0:1] = gain_ref[...].reshape(1, D)
    vec_t[1:2] = wg_ref[...].reshape(1, D)
    vec_p[...] = jnp.zeros(vec_p.shape, F32)
    steer_p[...] = jnp.zeros(steer_p.shape, BF16)
    for c in range(S // 2):
        cols = slice(c * 2 * rows, (c + 1) * 2 * rows)
        vec_p[c, :, : 2 * rows] = vec_t[:, cols]
        steer_p[c, :, : 2 * rows] = steer_ref[:, cols]
    gap = jnp.zeros((T, norm_c.shape[2] - rows), F32)

    def halves(value):
        low = jnp.concatenate([value[:, :rows], gap], axis=1)
        high = jnp.concatenate([value[:, rows : 2 * rows], gap], axis=1)
        return low.astype(BF16), high.astype(BF16)

    def pair_rows(value, c):
        fill = jnp.zeros((tok_p.shape[2] - 2 * rows, T), F32)
        return jnp.concatenate([value[c * 2 * rows : (c + 1) * 2 * rows], fill], axis=0).T

    loads["tok"].wait()
    tokens = tok_t[...].astype(F32)
    inverse = column(
        lax.rsqrt(jnp.sum(tokens * tokens, axis=0, keepdims=True) * (1.0 / D) + EPSILON)
    )
    gate_sum = jnp.zeros(tok_p.shape[1:], F32)
    for c in range(S // 2):
        part = pair_rows(tokens, c)
        tok_p[c] = part.astype(BF16)
        normed = (part * inverse * vec_p[c, 0:1]).astype(BF16).astype(F32)
        norm_c[2 * c], norm_c[2 * c + 1] = halves(normed)
        gate_sum = gate_sum + normed * vec_p[c, 1:2]
    gate = jax.nn.sigmoid(jnp.sum(gate_sum, axis=1, keepdims=True))

    def q_acc(slot):
        qacc[...] += dot(norm_c[slot], qbuf[slot])

    def q_sib(slot):
        for i in every:
            q_copy(slot, 2, i).wait_recv()
        q_acc(slot)

    def q_work(t):
        a, b = at(pos + C - t), at(pos + t)
        q_acc(a)
        q_acc(b)
        q_sib(a + other)
        q_sib(b + other)

    q_fwd(1)
    qacc[...] = dot(norm_c[me], qbuf[me])
    q_sib(sib)
    loads["go"].wait()
    grads = go_t[...].astype(F32)
    for c in range(S // 2):
        part = pair_rows(grads, c)
        go_p[c] = part.astype(BF16)
        go_c[2 * c], go_c[2 * c + 1] = halves(part)

    def q_both(t, carry):
        q_fwd(t)
        q_work(t - 1)
        return carry

    lax.fori_loop(2, half, q_both, 0)
    for i in every:
        for way in range(3):
            o_copy(me, way, i).start()
    q_work(half - 1)
    far = at(pos + half)
    for i in every:
        q_copy(far, 0, i).wait_recv()
        q_copy(far, 2, i).start()
    q_acc(far)
    q_sib(far + other)

    qkv = qacc[...].astype(BF16)
    kvall[T:] = qkv[:, group_cols:]
    kv_copy = remote(
        kvall.at[pl.ds(T, T)], kvall.at[pl.ds(0, T)], kvsem.at[0], kvsem.at[1], after, h
    )
    kv_copy.start()

    sidx_row = sidx_ref[...]
    sidx_col = column(sidx_row)
    one_hot_b = (
        (lax.broadcasted_iota(jnp.int32, (T, steer_count), 1) == sidx_col).astype(F32).astype(BF16)
    )
    one_hot_t = (lax.broadcasted_iota(jnp.int32, (steer_count, T), 0) == sidx_row).astype(F32)

    def logit_step(c, total):
        return total + go_p[c].astype(F32) * dot(one_hot_b, steer_p[c])

    logit_sum = lax.fori_loop(0, S // 2, logit_step, jnp.zeros(go_p.shape[1:], F32))
    grad_logit = gate * (1.0 - gate) * jnp.sum(logit_sum, axis=1, keepdims=True)

    @pl.loop(0, share)
    def _(j):
        sacc[0, j] = jnp.dot(
            one_hot_t,
            gate * go_p[h * share + j].astype(F32),
            precision=HIGHEST,
            preferred_element_type=F32,
        )

    def s_copy(k):
        return remote(sacc.at[k], srecv.at[k], ssend.at[k], srsem.at[k], pairs[k], h)

    def s_finish(k):
        s_copy(k).wait_recv()
        sacc[k + 1] = sacc[k] + srecv[k]

    s_copy(0).start()

    def gate_step(c, total):
        return total + vec_p[c, 1:2] * vec_p[c, 0:1] * tok_p[c].astype(F32)

    gate_terms = lax.fori_loop(0, S // 2, gate_step, jnp.zeros(go_p.shape[1:], F32))
    row_gate = grad_logit * inverse * jnp.sum(gate_terms, axis=1, keepdims=True)

    seg_copy.wait_recv()
    halo_seg = jnp.where(me > 0, segbuf[0, 0:1, :], -1)
    seg_row = seg_ref[...]
    query_seg = column(seg_row)
    key_seg = jnp.concatenate([halo_seg, seg_row], axis=1)
    distance = (
        lax.broadcasted_iota(jnp.int32, (T, 2 * T), 0)
        - lax.broadcasted_iota(jnp.int32, (T, 2 * T), 1)
        + T
    )
    mask = (distance >= 0) & (distance < WIN) & (query_seg == key_seg)

    kv_copy.wait_recv()
    keys = kvall[:, :hd]
    values = kvall[:, hd:]
    mixed_parts = []
    for i in range(heads):
        scores = dot_t(qkv[:, i * hd : (i + 1) * hd], keys) * scale
        scores = jnp.where(mask, scores, -1e30)
        raised = jnp.exp(scores - jnp.max(scores, axis=1, keepdims=True))
        probs = raised / jnp.sum(raised, axis=1, keepdims=True)
        pbuf[i] = probs
        mixed_parts.append(dot(probs.astype(BF16), values).astype(BF16))
        if i == heads // 2 - 1:
            o_fwd(1)
        if i == heads - 1:
            o_fwd(2)
    mixed = jnp.concatenate(mixed_parts, axis=1)

    def joined(low, high):
        fill = jnp.zeros((T, abuf.shape[2] - 2 * rows), F32)
        return jnp.concatenate([low[:, :rows], high[:, :rows], fill], axis=1).astype(BF16)

    def a_copy(pair):
        return remote(
            abuf.at[pair],
            arecv.at[h, pair % share],
            asend.at[pair],
            arsem.at[h, pair % share],
            me,
            pair // share,
        )

    def o_acc(slot):
        for i in every:
            o_copy(slot + other, 2, i).wait_recv()
        pair = slot // 2
        low, high = obuf[2 * pair], obuf[2 * pair + 1]
        abuf[pair] = joined(dot_t(mixed, low), dot_t(mixed, high))

        @pl.when(pair // share != h)
        def _():
            a_copy(pair).start()

        gmacc[...] += dot(go_c[2 * pair], low) + dot(go_c[2 * pair + 1], high)

    def o_work(t):
        o_acc(at(pos + t))
        o_acc(at(pos + C - t))

    gmacc[...] = jnp.zeros(gmacc.shape, F32)
    o_acc(me)
    o_work(1)

    def o_both(t, carry):
        o_fwd(t)
        o_work(t - 1)
        return carry

    lax.fori_loop(3, half, o_both, 0)
    for i in every:
        o_copy(far, 1, i).wait_recv()
        o_copy(far, 2, i).start()
    s_finish(0)
    s_copy(1).start()
    o_work(half - 1)
    o_acc(far)

    grad_mixed = gmacc[...].astype(BF16)
    grad_query = []
    grad_keys = jnp.zeros((2 * T, hd), F32)
    grad_values = jnp.zeros((2 * T, hd), F32)
    for i in range(heads):
        part = grad_mixed[:, i * hd : (i + 1) * hd]
        probs = pbuf[i]
        grad_prob = dot_t(part, values)
        delta = jnp.sum(probs * grad_prob, axis=1, keepdims=True)
        grad_scores = (probs * (grad_prob - delta) * scale).astype(BF16)
        grad_query.append(dot(grad_scores, keys).astype(BF16))
        grad_keys = grad_keys + t_dot(grad_scores, qkv[:, i * hd : (i + 1) * hd])
        grad_values = grad_values + t_dot(probs.astype(BF16), part)
    grad_kv = jnp.concatenate([grad_keys, grad_values], axis=1)
    hgsend[...] = grad_kv[:T].astype(BF16)
    hg_copy = remote(hgsend, hgrecv, hgsem.at[0], hgsem.at[1], before, h)
    hg_copy.start()
    s_finish(1)
    s_copy(2).start()

    for j in range(share):
        c = h * share + j
        total = abuf[c].astype(F32)
        for peer in peers:
            remote(
                abuf.at[c], arecv.at[peer, j], asend.at[c], arsem.at[peer, j], me, peer
            ).wait_recv()
            total = total + arecv[peer, j].astype(F32)
        steer_rows = dot(one_hot_b, steer_p[c])
        out = tok_p[c].astype(F32) + total + gate * steer_rows
        lay_ref[:, j * 2 * rows : (j + 1) * 2 * rows] = out[:, : 2 * rows].astype(BF16)

    s_finish(2)
    s_copy(3).start()
    hg_copy.wait_recv()
    kv_back = (grad_kv[T:] + hgrecv[...].astype(F32)).astype(BF16)
    grad_all = jnp.concatenate(grad_query + [kv_back], axis=1)

    def g_copy(pair):
        return remote(
            gbuf.at[pair],
            grecv.at[h, pair % share],
            gsend.at[pair],
            grsem.at[h, pair % share],
            me,
            pair // share,
        )

    def g_step(i, total):
        c = ((h + 1) * share + i) % (S // 2)
        term = joined(dot_t(grad_all, qbuf[2 * c]), dot_t(grad_all, qbuf[2 * c + 1]))
        gbuf[c] = term

        @pl.when(c // share != h)
        def _():
            g_copy(c).start()

        return total + term.astype(F32) * vec_p[c, 0:1] * tok_p[c].astype(F32)

    row_terms = lax.fori_loop(0, S // 2, g_step, jnp.zeros(go_p.shape[1:], F32))
    row_own = jnp.sum(row_terms, axis=1, keepdims=True) * inverse
    as_row = jnp.sum(jnp.where(same, jnp.broadcast_to(row_own, (T, T)), 0.0), axis=0, keepdims=True)
    rbuf[...] = jnp.broadcast_to(as_row, rbuf.shape)

    def r_copy(d):
        return remote(rbuf, rrecv.at[h], rsend.at[d], rrsem.at[h], me, peers[d])

    for d in range(H - 1):
        r_copy(d).start()
    for k in range(3, steps):
        s_finish(k)
        if k + 1 < steps:
            s_copy(k + 1).start()

    row_total = row_own + row_gate
    for j in range(share):
        sgrad_ref[:, j * 2 * rows : (j + 1) * 2 * rows] = sacc[steps, j][:, : 2 * rows]
    for peer in peers:
        remote(rbuf, rrecv.at[peer], rsend.at[0], rrsem.at[peer], me, peer).wait_recv()
        row_total = row_total + column(rrecv[peer, 0:1, :])
    row_mean = row_total * (1.0 / D)

    for j in range(share):
        c = h * share + j
        total = gbuf[c].astype(F32)
        for peer in peers:
            remote(
                gbuf.at[c], grecv.at[peer, j], gsend.at[c], grsem.at[peer, j], me, peer
            ).wait_recv()
            total = total + grecv[peer, j].astype(F32)
        scaled = (total + grad_logit * vec_p[c, 1:2]) * vec_p[c, 0:1]
        unit = tok_p[c].astype(F32) * inverse
        out = go_p[c].astype(F32) + inverse * (scaled - unit * row_mean)
        gtok_ref[:, j * 2 * rows : (j + 1) * 2 * rows] = out[:, : 2 * rows].astype(BF16)

    seg_copy.wait_send()
    kv_copy.wait_send()
    hg_copy.wait_send()
    for k in range(steps):
        s_copy(k).wait_send()
    for d in range(H - 1):
        r_copy(d).wait_send()

    def sent(i, carry):
        c = ((h + 1) * share + i) % (S // 2)
        a_copy(c).wait_send()
        g_copy(c).wait_send()
        return carry

    lax.fori_loop(0, S // 2 - share, sent, 0)
    for i in every:
        for way in range(3):
            q_copy(me, way, i).wait_send()
            o_copy(me, way, i).wait_send()

    def ring_sent(t, carry):
        a, b = at(pos + C - t), at(pos + t)
        for i in every:
            q_copy(a, 0, i).wait_send()
            o_copy(b, 1, i).wait_send()

            @pl.when(t < half - 1)
            def _():
                q_copy(b, 1, i).wait_send()
                o_copy(a, 0, i).wait_send()

            for slot in (a, b):
                q_copy(slot, 2, i).wait_send()
                o_copy(slot, 2, i).wait_send()
        return carry

    lax.fori_loop(1, half, ring_sent, 0)
    for i in every:
        q_copy(far, 2, i).wait_send()
        o_copy(far, 2, i).wait_send()


def shards(
    S,
    H,
    tokens,
    gain,
    w_query,
    w_key,
    w_value,
    w_out,
    w_gate,
    steering,
    segment_ids,
    steer_index,
    grad_out,
):
    T, D = tokens.shape
    rows, group_cols = w_query.shape
    hd = w_key.shape[1]
    heads = group_cols // hd
    wide = group_cols + 2 * hd
    pad = -(-rows // (16 * PIECES)) * 16 * PIECES
    pairs = S // H // 2
    pair_wide = -(-2 * rows // 128) * 128
    steps = S.bit_length() - 1
    steer_count = steering.shape[0]
    dma = pltpu.SemaphoreType.DMA
    vmem = pltpu.VMEM
    scratch = [
        vmem((S, pad, wide), BF16),
        vmem((S, pad, group_cols), BF16),
        vmem((D, T), BF16),
        vmem((D,), F32),
        vmem((D,), F32),
        vmem((rows, group_cols), BF16),
        vmem((hd, rows), BF16),
        vmem((hd, rows), BF16),
        vmem((rows, group_cols), BF16),
        vmem((steer_count, D), BF16),
        vmem((1, T), jnp.int32),
        vmem((1, T), jnp.int32),
        vmem((D, T), BF16),
        vmem((2 * hd, -(-rows // 128) * 128), F32),
        vmem((2, D), F32),
        vmem((S // 2, T, pair_wide), BF16),
        vmem((S // 2, T, pair_wide), BF16),
        vmem((S, T, pad), BF16),
        vmem((S, T, pad), BF16),
        vmem((S // 2, 2, pair_wide), F32),
        vmem((S // 2, steer_count, pair_wide), BF16),
        vmem((T, wide), F32),
        vmem((T, group_cols), F32),
        vmem((2 * T, 2 * hd), BF16),
        vmem((2, 8, T), jnp.int32),
        vmem((heads, T, 2 * T), F32),
        vmem((S // 2, T, pair_wide), BF16),
        vmem((H, pairs, T, pair_wide), BF16),
        vmem((S // 2, T, pair_wide), BF16),
        vmem((H, pairs, T, pair_wide), BF16),
        vmem((8, T), F32),
        vmem((H, 8, T), F32),
        vmem((T, 2 * hd), BF16),
        vmem((T, 2 * hd), BF16),
        vmem((steps + 1, pairs, steer_count, pair_wide), F32),
        vmem((steps, pairs, steer_count, pair_wide), F32),
        dma((3, S, PIECES)),
        dma((S, PIECES)),
        dma((3, S, PIECES)),
        dma((S, PIECES)),
        dma((2,)),
        dma((2,)),
        dma((2,)),
        dma((S // 2,)),
        dma((H, pairs)),
        dma((S // 2,)),
        dma((H, pairs)),
        dma((max(H - 1, 1),)),
        dma((H,)),
        dma((steps,)),
        dma((steps,)),
        dma((11,)),
    ]
    far_off = pl.BlockSpec(memory_space=pl.ANY)
    return pl.pallas_call(
        functools.partial(kernel, S, H),
        out_shape=(
            jax.ShapeDtypeStruct((T, D // H), BF16),
            jax.ShapeDtypeStruct((T, D // H), BF16),
            jax.ShapeDtypeStruct((steer_count, D // H), F32),
        ),
        in_specs=[far_off] * 11,
        out_specs=[pl.BlockSpec(memory_space=pltpu.VMEM)] * 3,
        scratch_shapes=scratch,
        compiler_params=pltpu.CompilerParams(
            collective_id=0, has_side_effects=True, vmem_limit_bytes=60 * 1024 * 1024
        ),
    )(
        tokens.T,
        gain,
        w_gate,
        w_query,
        w_key.T,
        w_value.T,
        w_out,
        steering,
        segment_ids.reshape(1, T),
        steer_index.reshape(1, T),
        grad_out.T,
    )


def solution(mesh):
    placed = (
        P("seq", None),
        P(),
        P("seq", "head"),
        P("seq", "head"),
        P("seq", "head"),
        P("seq", "head"),
        P(),
        P(),
        P("seq"),
        P("seq"),
        P("seq", None),
    )
    return jax.shard_map(
        functools.partial(shards, mesh.shape["seq"], mesh.shape["head"]),
        mesh=mesh,
        in_specs=placed,
        out_specs=(P("seq", "head"), P("seq", "head"), P(None, "head")),
        check_vma=False,
    )
```

```python
import functools
import jax
import jax.numpy as jnp
from jax import lax
from jax.experimental import pallas as pl
from jax.experimental.pallas import tpu as pltpu
from jax.sharding import PartitionSpec as P

WIN = 128
EPSILON = 1e-05
HIGHEST = lax.Precision.HIGHEST
MESH = pl.DeviceIdType.MESH
PIECES = 3
ROWS_OF_CHIPS = 4
F32 = jnp.float32
BF16 = jnp.bfloat16


def dot(left, right):
    return jnp.dot(left, right, preferred_element_type=F32)


def dot_t(left, right):
    return lax.dot_general(left, right, (((1,), (1,)), ((), ())), preferred_element_type=F32)


def t_dot(left, right):
    return lax.dot_general(left, right, (((0,), (0,)), ((), ())), preferred_element_type=F32)


def kernel(
    S,
    H,
    tok_any,
    gain_any,
    wg_any,
    wq_any,
    wk_any,
    wv_any,
    wo_any,
    steer_any,
    seg_any,
    sidx_any,
    go_any,
    lay_ref,
    gtok_ref,
    sgrad_ref,
    qbuf,
    obuf,
    tok_t,
    gain_ref,
    wg_ref,
    wq_ref,
    wk_ref,
    wv_ref,
    wo_ref,
    steer_ref,
    seg_ref,
    sidx_ref,
    go_t,
    kv_t,
    vec_t,
    tok_p,
    go_p,
    go_c,
    norm_c,
    vec_p,
    steer_p,
    qacc,
    gmacc,
    kvall,
    segbuf,
    pbuf,
    abuf,
    arecv,
    gbuf,
    grecv,
    rbuf,
    rrecv,
    hgsend,
    hgrecv,
    sacc,
    srecv,
    qsend,
    qrecv,
    osend,
    orecv,
    segsem,
    kvsem,
    hgsem,
    asend,
    arsem,
    gsend,
    grsem,
    rsend,
    rrsem,
    ssend,
    srsem,
    loadsem,
    out_t,
):
    D, T = tok_any.shape
    rows, group_cols = wq_ref.shape
    hd = wk_ref.shape[0]
    heads = group_cols // hd
    scale = hd ** (-0.5)
    share = S // H // 2
    C = S // 2
    half = C // 2
    Y = C // ROWS_OF_CHIPS
    steps = sacc.shape[0] - 1
    steer_count = steer_ref.shape[0]

    me = lax.axis_index("seq")
    h = lax.axis_index("head")
    core = me % 2
    chip = me // 2
    z, y = chip // Y, chip % Y
    odd = z % 2
    inner = z * (Y - 1) + (1 - odd) * (y - 1) + odd * (Y - 1 - y)
    outer = ROWS_OF_CHIPS * (Y - 1) + (ROWS_OF_CHIPS - 1 - z)
    pos = jnp.where(y == 0, outer, inner)

    def at(place):
        p = place % C
        zi = p // (Y - 1)
        o = p % (Y - 1)
        yi = jnp.where(zi % 2 == 0, 1 + o, Y - 1 - o)
        last = p >= ROWS_OF_CHIPS * (Y - 1)
        zz = jnp.where(last, ROWS_OF_CHIPS - 1 - (p - ROWS_OF_CHIPS * (Y - 1)), zi)
        yy = jnp.where(last, 0, yi)
        return (zz * Y + yy) * 2 + core

    cw, ccw = at(pos + 1), at(pos + C - 1)
    other = 1 - 2 * core
    sib = me + other
    after, before = (me + 1) % S, (me + S - 1) % S
    pairs = []
    for k in range(steps):
        bit = (me // (1 << k)) % 2
        pairs.append(me + (1 - 2 * bit) * (1 << k))
    peers = [(h + d) % H for d in range(1, H)]

    loads = {}
    for i, (name, src, dst) in enumerate(
        [
            ("wq", wq_any, wq_ref),
            ("wk", wk_any, wk_ref),
            ("wv", wv_any, wv_ref),
            ("wo", wo_any, wo_ref),
            ("seg", seg_any, seg_ref),
            ("tok", tok_any, tok_t),
            ("gain", gain_any, gain_ref),
            ("wg", wg_any, wg_ref),
            ("steer", steer_any, steer_ref),
            ("sidx", sidx_any, sidx_ref),
            ("go", go_any, go_t),
        ]
    ):
        loads[name] = pltpu.make_async_copy(src, dst, loadsem.at[i])
        loads[name].start()

    barrier = pltpu.get_barrier_semaphore()
    for target in [cw, ccw, sib, after, before] + pairs:
        pl.semaphore_signal(barrier, inc=1, device_id=(target, h), device_id_type=MESH)
    for peer in peers:
        pl.semaphore_signal(barrier, inc=1, device_id=(me, peer), device_id_type=MESH)

    qbuf[me] = jnp.zeros(qbuf.shape[1:], BF16)
    obuf[me] = jnp.zeros(obuf.shape[1:], BF16)
    kv_t[...] = jnp.zeros(kv_t.shape, F32)
    for name in ("wq", "wk", "wv", "wo", "seg"):
        loads[name].wait()
    qbuf[me, :rows, :group_cols] = wq_ref[...]
    kv_t[:hd, :rows] = wk_ref[...].astype(F32)
    kv_t[hd:, :rows] = wv_ref[...].astype(F32)
    qbuf[me, :rows, group_cols:] = kv_t[...].T[:rows].astype(BF16)
    obuf[me, :rows, :] = wo_ref[...]
    segbuf[1] = jnp.broadcast_to(seg_ref[...], segbuf.shape[1:])

    pl.semaphore_wait(barrier, 5 + steps + H - 1)

    def remote(src, dst, send, recv, seq, head):
        return pltpu.make_async_remote_copy(
            src_ref=src,
            dst_ref=dst,
            send_sem=send,
            recv_sem=recv,
            device_id=(seq, head),
            device_id_type=MESH,
        )

    targets = (cw, ccw, sib)
    piece = qbuf.shape[1] // PIECES

    def q_copy(slot, way, i):
        part = pl.ds(i * piece, piece)
        return remote(
            qbuf.at[slot, part],
            qbuf.at[slot, part],
            qsend.at[way, slot, i],
            qrecv.at[slot, i],
            targets[way],
            h,
        )

    def o_copy(slot, way, i):
        part = pl.ds(i * piece, piece)
        return remote(
            obuf.at[slot, part],
            obuf.at[slot, part],
            osend.at[way, slot, i],
            orecv.at[slot, i],
            targets[way],
            h,
        )

    every = range(PIECES)
    for i in every:
        for way in range(3):
            q_copy(me, way, i).start()
    seg_copy = remote(segbuf.at[1], segbuf.at[0], segsem.at[0], segsem.at[1], after, h)
    seg_copy.start()

    def q_fwd(t):
        a, b = at(pos + C - t), at(pos + t)
        for i in every:
            q_copy(a, 0, i).wait_recv()
            q_copy(a, 0, i).start()
            q_copy(a, 2, i).start()
            q_copy(b, 1, i).wait_recv()

            @pl.when(t < half - 1)
            def _():
                q_copy(b, 1, i).start()

            q_copy(b, 2, i).start()

    def o_fwd(t):
        b, a = at(pos + t), at(pos + C - t)
        for i in every:
            o_copy(b, 1, i).wait_recv()
            o_copy(b, 1, i).start()
            o_copy(b, 2, i).start()
            o_copy(a, 0, i).wait_recv()

            @pl.when(t < half - 1)
            def _():
                o_copy(a, 0, i).start()

            o_copy(a, 2, i).start()

    same = lax.broadcasted_iota(jnp.int32, (T, T), 0) == lax.broadcasted_iota(jnp.int32, (T, T), 1)

    def column(row):
        return jnp.sum(
            jnp.where(same, jnp.broadcast_to(row, (T, T)), 0), axis=1, keepdims=True
        )

    for name in ("gain", "wg", "steer", "sidx"):
        loads[name].wait()
    vec_t[0:1] = gain_ref[...].reshape(1, D)
    vec_t[1:2] = wg_ref[...].reshape(1, D)
    vec_p[...] = jnp.zeros(vec_p.shape, F32)
    steer_p[...] = jnp.zeros(steer_p.shape, BF16)
    for c in range(S // 2):
        cols = slice(c * 2 * rows, (c + 1) * 2 * rows)
        vec_p[c, :, : 2 * rows] = vec_t[:, cols]
        steer_p[c, :, : 2 * rows] = steer_ref[:, cols]
    gap = jnp.zeros((T, norm_c.shape[2] - rows), F32)

    def halves(value):
        low = jnp.concatenate([value[:, :rows], gap], axis=1)
        high = jnp.concatenate([value[:, rows : 2 * rows], gap], axis=1)
        return low.astype(BF16), high.astype(BF16)

    def pair_rows(value, c):
        fill = jnp.zeros((tok_p.shape[2] - 2 * rows, T), F32)
        return jnp.concatenate([value[c * 2 * rows : (c + 1) * 2 * rows], fill], axis=0).T

    loads["tok"].wait()
    tokens = tok_t[...].astype(F32)
    inverse = column(
        lax.rsqrt(jnp.sum(tokens * tokens, axis=0, keepdims=True) * (1.0 / D) + EPSILON)
    )
    gate_sum = jnp.zeros(tok_p.shape[1:], F32)
    for c in range(S // 2):
        part = pair_rows(tokens, c)
        tok_p[c] = part.astype(BF16)
        normed = (part * inverse * vec_p[c, 0:1]).astype(BF16).astype(F32)
        norm_c[2 * c], norm_c[2 * c + 1] = halves(normed)
        gate_sum = gate_sum + normed * vec_p[c, 1:2]
    gate = jax.nn.sigmoid(jnp.sum(gate_sum, axis=1, keepdims=True))

    def q_acc(slot):
        qacc[...] += dot(norm_c[slot], qbuf[slot])

    def q_sib(slot):
        for i in every:
            q_copy(slot, 2, i).wait_recv()
        q_acc(slot)

    def q_work(t):
        a, b = at(pos + C - t), at(pos + t)
        q_acc(a)
        q_acc(b)
        q_sib(a + other)
        q_sib(b + other)

    q_fwd(1)
    qacc[...] = dot(norm_c[me], qbuf[me])
    q_sib(sib)
    loads["go"].wait()
    grads = go_t[...].astype(F32)
    for c in range(S // 2):
        part = pair_rows(grads, c)
        go_p[c] = part.astype(BF16)
        go_c[2 * c], go_c[2 * c + 1] = halves(part)

    def q_both(t, carry):
        q_fwd(t)
        q_work(t - 1)
        return carry

    lax.fori_loop(2, half, q_both, 0)
    for i in every:
        for way in range(3):
            o_copy(me, way, i).start()
    q_work(half - 1)
    far = at(pos + half)
    for i in every:
        q_copy(far, 0, i).wait_recv()
        q_copy(far, 2, i).start()
    q_acc(far)
    q_sib(far + other)

    qkv = qacc[...].astype(BF16)
    kvall[T:] = qkv[:, group_cols:]
    kv_copy = remote(
        kvall.at[pl.ds(T, T)], kvall.at[pl.ds(0, T)], kvsem.at[0], kvsem.at[1], after, h
    )
    kv_copy.start()

    sidx_row = sidx_ref[...]
    sidx_col = column(sidx_row)
    one_hot_b = (
        (lax.broadcasted_iota(jnp.int32, (T, steer_count), 1) == sidx_col).astype(F32).astype(BF16)
    )
    one_hot_t = (lax.broadcasted_iota(jnp.int32, (steer_count, T), 0) == sidx_row).astype(F32)

    def logit_step(c, total):
        return total + go_p[c].astype(F32) * dot(one_hot_b, steer_p[c])

    logit_sum = lax.fori_loop(0, S // 2, logit_step, jnp.zeros(go_p.shape[1:], F32))
    grad_logit = gate * (1.0 - gate) * jnp.sum(logit_sum, axis=1, keepdims=True)

    @pl.loop(0, share)
    def _(j):
        sacc[0, j] = jnp.dot(
            one_hot_t,
            gate * go_p[h * share + j].astype(F32),
            precision=HIGHEST,
            preferred_element_type=F32,
        )

    def s_copy(k):
        return remote(sacc.at[k], srecv.at[k], ssend.at[k], srsem.at[k], pairs[k], h)

    def s_finish(k):
        s_copy(k).wait_recv()
        sacc[k + 1] = sacc[k] + srecv[k]

    s_copy(0).start()

    def gate_step(c, total):
        return total + vec_p[c, 1:2] * vec_p[c, 0:1] * tok_p[c].astype(F32)

    gate_terms = lax.fori_loop(0, S // 2, gate_step, jnp.zeros(go_p.shape[1:], F32))
    row_gate = grad_logit * inverse * jnp.sum(gate_terms, axis=1, keepdims=True)

    seg_copy.wait_recv()
    halo_seg = jnp.where(me > 0, segbuf[0, 0:1, :], -1)
    seg_row = seg_ref[...]
    query_seg = column(seg_row)
    key_seg = jnp.concatenate([halo_seg, seg_row], axis=1)
    distance = (
        lax.broadcasted_iota(jnp.int32, (T, 2 * T), 0)
        - lax.broadcasted_iota(jnp.int32, (T, 2 * T), 1)
        + T
    )
    mask = (distance >= 0) & (distance < WIN) & (query_seg == key_seg)

    kv_copy.wait_recv()
    keys = kvall[:, :hd]
    values = kvall[:, hd:]
    mixed_parts = []
    for i in range(heads):
        scores = dot_t(qkv[:, i * hd : (i + 1) * hd], keys) * scale
        scores = jnp.where(mask, scores, -1e30)
        raised = jnp.exp(scores - jnp.max(scores, axis=1, keepdims=True))
        probs = raised / jnp.sum(raised, axis=1, keepdims=True)
        pbuf[i] = probs
        mixed_parts.append(dot(probs.astype(BF16), values).astype(BF16))
        if i == heads // 2 - 1:
            o_fwd(1)
        if i == heads - 1:
            o_fwd(2)
    mixed_t = jnp.concatenate(mixed_parts, axis=1).astype(F32).T.astype(BF16)

    def joined(low, high):
        fill = jnp.zeros((abuf.shape[2] - 2 * rows, T), F32)
        return jnp.concatenate([low[:rows], high[:rows], fill], axis=0).T.astype(BF16)

    def a_copy(pair):
        return remote(
            abuf.at[pair],
            arecv.at[h, pair % share],
            asend.at[pair],
            arsem.at[h, pair % share],
            me,
            pair // share,
        )

    def o_acc(slot):
        for i in every:
            o_copy(slot + other, 2, i).wait_recv()
        pair = slot // 2
        low, high = obuf[2 * pair], obuf[2 * pair + 1]
        abuf[pair] = joined(dot(low, mixed_t), dot(high, mixed_t))

        @pl.when(pair // share != h)
        def _():
            a_copy(pair).start()

        gmacc[...] += dot(go_c[2 * pair], low) + dot(go_c[2 * pair + 1], high)

    def o_work(t):
        o_acc(at(pos + t))
        o_acc(at(pos + C - t))

    gmacc[...] = jnp.zeros(gmacc.shape, F32)
    o_acc(me)
    o_work(1)

    def o_both(t, carry):
        o_fwd(t)
        o_work(t - 1)
        return carry

    lax.fori_loop(3, half, o_both, 0)
    for i in every:
        o_copy(far, 1, i).wait_recv()
        o_copy(far, 2, i).start()
    s_finish(0)
    s_copy(1).start()
    o_work(half - 1)
    o_acc(far)

    grad_mixed = gmacc[...].astype(BF16)
    grad_query = []
    grad_keys = jnp.zeros((2 * T, hd), F32)
    grad_values = jnp.zeros((2 * T, hd), F32)
    for i in range(heads):
        part = grad_mixed[:, i * hd : (i + 1) * hd]
        probs = pbuf[i]
        grad_prob = dot_t(part, values)
        delta = jnp.sum(probs * grad_prob, axis=1, keepdims=True)
        grad_scores = (probs * (grad_prob - delta) * scale).astype(BF16)
        grad_query.append(dot(grad_scores, keys).astype(BF16))
        grad_keys = grad_keys + t_dot(grad_scores, qkv[:, i * hd : (i + 1) * hd])
        grad_values = grad_values + t_dot(probs.astype(BF16), part)
    grad_kv = jnp.concatenate([grad_keys, grad_values], axis=1)
    hgsend[...] = grad_kv[:T].astype(BF16)
    hg_copy = remote(hgsend, hgrecv, hgsem.at[0], hgsem.at[1], before, h)
    hg_copy.start()
    s_finish(1)
    s_copy(2).start()

    for j in range(share):
        c = h * share + j
        total = abuf[c].astype(F32)
        for peer in peers:
            remote(
                abuf.at[c], arecv.at[peer, j], asend.at[c], arsem.at[peer, j], me, peer
            ).wait_recv()
            total = total + arecv[peer, j].astype(F32)
        steer_rows = dot(one_hot_b, steer_p[c])
        out = tok_p[c].astype(F32) + total + gate * steer_rows
        out_t[j * 2 * rows : (j + 1) * 2 * rows] = out.T[: 2 * rows]
    lay_ref[...] = out_t[...].astype(BF16)

    s_finish(2)
    s_copy(3).start()
    hg_copy.wait_recv()
    kv_back = (grad_kv[T:] + hgrecv[...].astype(F32)).astype(BF16)
    grad_t = jnp.concatenate(grad_query + [kv_back], axis=1).astype(F32).T.astype(BF16)

    def g_copy(pair):
        return remote(
            gbuf.at[pair],
            grecv.at[h, pair % share],
            gsend.at[pair],
            grsem.at[h, pair % share],
            me,
            pair // share,
        )

    def g_step(i, total):
        c = ((h + 1) * share + i) % (S // 2)
        term = joined(dot(qbuf[2 * c], grad_t), dot(qbuf[2 * c + 1], grad_t))
        gbuf[c] = term

        @pl.when(c // share != h)
        def _():
            g_copy(c).start()

        return total + term.astype(F32) * vec_p[c, 0:1] * tok_p[c].astype(F32)

    row_terms = lax.fori_loop(0, S // 2, g_step, jnp.zeros(go_p.shape[1:], F32))
    row_own = jnp.sum(row_terms, axis=1, keepdims=True) * inverse
    as_row = jnp.sum(jnp.where(same, jnp.broadcast_to(row_own, (T, T)), 0.0), axis=0, keepdims=True)
    rbuf[...] = jnp.broadcast_to(as_row, rbuf.shape)

    def r_copy(d):
        return remote(rbuf, rrecv.at[h], rsend.at[d], rrsem.at[h], me, peers[d])

    for d in range(H - 1):
        r_copy(d).start()
    for k in range(3, steps):
        s_finish(k)
        if k + 1 < steps:
            s_copy(k + 1).start()

    row_total = row_own + row_gate
    for j in range(share):
        sgrad_ref[:, j * 2 * rows : (j + 1) * 2 * rows] = sacc[steps, j][:, : 2 * rows]
    for peer in peers:
        remote(rbuf, rrecv.at[peer], rsend.at[0], rrsem.at[peer], me, peer).wait_recv()
        row_total = row_total + column(rrecv[peer, 0:1, :])
    row_mean = row_total * (1.0 / D)

    for j in range(share):
        c = h * share + j
        total = gbuf[c].astype(F32)
        for peer in peers:
            remote(
                gbuf.at[c], grecv.at[peer, j], gsend.at[c], grsem.at[peer, j], me, peer
            ).wait_recv()
            total = total + grecv[peer, j].astype(F32)
        scaled = (total + grad_logit * vec_p[c, 1:2]) * vec_p[c, 0:1]
        unit = tok_p[c].astype(F32) * inverse
        out = go_p[c].astype(F32) + inverse * (scaled - unit * row_mean)
        out_t[j * 2 * rows : (j + 1) * 2 * rows] = out.T[: 2 * rows]
    gtok_ref[...] = out_t[...].astype(BF16)

    seg_copy.wait_send()
    kv_copy.wait_send()
    hg_copy.wait_send()
    for k in range(steps):
        s_copy(k).wait_send()
    for d in range(H - 1):
        r_copy(d).wait_send()

    def sent(i, carry):
        c = ((h + 1) * share + i) % (S // 2)
        a_copy(c).wait_send()
        g_copy(c).wait_send()
        return carry

    lax.fori_loop(0, S // 2 - share, sent, 0)
    for i in every:
        for way in range(3):
            q_copy(me, way, i).wait_send()
            o_copy(me, way, i).wait_send()

    def ring_sent(t, carry):
        a, b = at(pos + C - t), at(pos + t)
        for i in every:
            q_copy(a, 0, i).wait_send()
            o_copy(b, 1, i).wait_send()

            @pl.when(t < half - 1)
            def _():
                q_copy(b, 1, i).wait_send()
                o_copy(a, 0, i).wait_send()

            for slot in (a, b):
                q_copy(slot, 2, i).wait_send()
                o_copy(slot, 2, i).wait_send()
        return carry

    lax.fori_loop(1, half, ring_sent, 0)
    for i in every:
        q_copy(far, 2, i).wait_send()
        o_copy(far, 2, i).wait_send()


def shards(
    S,
    H,
    tokens,
    gain,
    w_query,
    w_key,
    w_value,
    w_out,
    w_gate,
    steering,
    segment_ids,
    steer_index,
    grad_out,
):
    T, D = tokens.shape
    rows, group_cols = w_query.shape
    hd = w_key.shape[1]
    heads = group_cols // hd
    wide = group_cols + 2 * hd
    pad = -(-rows // (16 * PIECES)) * 16 * PIECES
    pairs = S // H // 2
    pair_wide = -(-2 * rows // 128) * 128
    steps = S.bit_length() - 1
    steer_count = steering.shape[0]
    dma = pltpu.SemaphoreType.DMA
    vmem = pltpu.VMEM
    scratch = [
        vmem((S, pad, wide), BF16),
        vmem((S, pad, group_cols), BF16),
        vmem((D, T), BF16),
        vmem((D,), F32),
        vmem((D,), F32),
        vmem((rows, group_cols), BF16),
        vmem((hd, rows), BF16),
        vmem((hd, rows), BF16),
        vmem((rows, group_cols), BF16),
        vmem((steer_count, D), BF16),
        vmem((1, T), jnp.int32),
        vmem((1, T), jnp.int32),
        vmem((D, T), BF16),
        vmem((2 * hd, -(-rows // 128) * 128), F32),
        vmem((2, D), F32),
        vmem((S // 2, T, pair_wide), BF16),
        vmem((S // 2, T, pair_wide), BF16),
        vmem((S, T, pad), BF16),
        vmem((S, T, pad), BF16),
        vmem((S // 2, 2, pair_wide), F32),
        vmem((S // 2, steer_count, pair_wide), BF16),
        vmem((T, wide), F32),
        vmem((T, group_cols), F32),
        vmem((2 * T, 2 * hd), BF16),
        vmem((2, 8, T), jnp.int32),
        vmem((heads, T, 2 * T), F32),
        vmem((S // 2, T, pair_wide), BF16),
        vmem((H, pairs, T, pair_wide), BF16),
        vmem((S // 2, T, pair_wide), BF16),
        vmem((H, pairs, T, pair_wide), BF16),
        vmem((8, T), F32),
        vmem((H, 8, T), F32),
        vmem((T, 2 * hd), BF16),
        vmem((T, 2 * hd), BF16),
        vmem((steps + 1, pairs, steer_count, pair_wide), F32),
        vmem((steps, pairs, steer_count, pair_wide), F32),
        dma((3, S, PIECES)),
        dma((S, PIECES)),
        dma((3, S, PIECES)),
        dma((S, PIECES)),
        dma((2,)),
        dma((2,)),
        dma((2,)),
        dma((S // 2,)),
        dma((H, pairs)),
        dma((S // 2,)),
        dma((H, pairs)),
        dma((max(H - 1, 1),)),
        dma((H,)),
        dma((steps,)),
        dma((steps,)),
        dma((11,)),
        vmem((D // H, T), F32),
    ]
    far_off = pl.BlockSpec(memory_space=pl.ANY)
    layer_t, grad_t, steer_grad = pl.pallas_call(
        functools.partial(kernel, S, H),
        out_shape=(
            jax.ShapeDtypeStruct((D // H, T), BF16),
            jax.ShapeDtypeStruct((D // H, T), BF16),
            jax.ShapeDtypeStruct((steer_count, D // H), F32),
        ),
        in_specs=[far_off] * 11,
        out_specs=[pl.BlockSpec(memory_space=pltpu.VMEM)] * 3,
        scratch_shapes=scratch,
        compiler_params=pltpu.CompilerParams(
            collective_id=0, has_side_effects=True, vmem_limit_bytes=60 * 1024 * 1024
        ),
    )(
        tokens.T,
        gain,
        w_gate,
        w_query,
        w_key.T,
        w_value.T,
        w_out,
        steering,
        segment_ids.reshape(1, T),
        steer_index.reshape(1, T),
        grad_out.T,
    )
    return layer_t.T, grad_t.T, steer_grad


def solution(mesh):
    placed = (
        P("seq", None),
        P(),
        P("seq", "head"),
        P("seq", "head"),
        P("seq", "head"),
        P("seq", "head"),
        P(),
        P(),
        P("seq"),
        P("seq"),
        P("seq", None),
    )
    return jax.shard_map(
        functools.partial(shards, mesh.shape["seq"], mesh.shape["head"]),
        mesh=mesh,
        in_specs=placed,
        out_specs=(P("seq", "head"), P("seq", "head"), P(None, "head")),
        check_vma=False,
    )
```

```python
import functools
import jax
import jax.numpy as jnp
from jax import lax
from jax.experimental import pallas as pl
from jax.experimental.pallas import tpu as pltpu
from jax.sharding import PartitionSpec as P

WIN = 128
EPSILON = 1e-05
HIGHEST = lax.Precision.HIGHEST
MESH = pl.DeviceIdType.MESH
PIECES = 3
ROWS_OF_CHIPS = 4
F32 = jnp.float32
BF16 = jnp.bfloat16


def dot(left, right):
    return jnp.dot(left, right, preferred_element_type=F32)


def dot_t(left, right):
    return lax.dot_general(left, right, (((1,), (1,)), ((), ())), preferred_element_type=F32)


def t_dot(left, right):
    return lax.dot_general(left, right, (((0,), (0,)), ((), ())), preferred_element_type=F32)


def kernel(
    S,
    H,
    tok_any,
    gain_any,
    wg_any,
    wq_any,
    wk_any,
    wv_any,
    wo_any,
    steer_any,
    seg_any,
    sidx_any,
    go_any,
    lay_ref,
    gtok_ref,
    sgrad_ref,
    qbuf,
    obuf,
    tok_t,
    gain_ref,
    wg_ref,
    wq_ref,
    wk_ref,
    wv_ref,
    wo_ref,
    steer_ref,
    seg_ref,
    sidx_ref,
    go_t,
    kv_t,
    vec_t,
    tok_p,
    go_p,
    go_c,
    norm_c,
    vec_p,
    steer_p,
    qacc,
    gmacc,
    kvall,
    segbuf,
    pbuf,
    abuf,
    arecv,
    gbuf,
    grecv,
    rbuf,
    rrecv,
    hgsend,
    hgrecv,
    sacc,
    srecv,
    qsend,
    qrecv,
    osend,
    orecv,
    segsem,
    kvsem,
    hgsem,
    asend,
    arsem,
    gsend,
    grsem,
    rsend,
    rrsem,
    ssend,
    srsem,
    loadsem,
    out_t,
):
    D, T = tok_any.shape
    rows, group_cols = wq_ref.shape
    hd = wk_ref.shape[0]
    heads = group_cols // hd
    scale = hd ** (-0.5)
    share = S // H // 2
    C = S // 2
    half = C // 2
    Y = C // ROWS_OF_CHIPS
    steps = sacc.shape[0] - 1
    steer_count = steer_ref.shape[0]

    me = lax.axis_index("seq")
    h = lax.axis_index("head")
    core = me % 2
    chip = me // 2
    z, y = chip // Y, chip % Y
    odd = z % 2
    inner = z * (Y - 1) + (1 - odd) * (y - 1) + odd * (Y - 1 - y)
    outer = ROWS_OF_CHIPS * (Y - 1) + (ROWS_OF_CHIPS - 1 - z)
    pos = jnp.where(y == 0, outer, inner)

    def at(place):
        p = place % C
        zi = p // (Y - 1)
        o = p % (Y - 1)
        yi = jnp.where(zi % 2 == 0, 1 + o, Y - 1 - o)
        last = p >= ROWS_OF_CHIPS * (Y - 1)
        zz = jnp.where(last, ROWS_OF_CHIPS - 1 - (p - ROWS_OF_CHIPS * (Y - 1)), zi)
        yy = jnp.where(last, 0, yi)
        return (zz * Y + yy) * 2 + core

    cw, ccw = at(pos + 1), at(pos + C - 1)
    other = 1 - 2 * core
    sib = me + other
    after, before = (me + 1) % S, (me + S - 1) % S
    pairs = []
    for k in range(steps):
        bit = (me // (1 << k)) % 2
        pairs.append(me + (1 - 2 * bit) * (1 << k))
    peers = [(h + d) % H for d in range(1, H)]

    loads = {}
    for i, (name, src, dst) in enumerate(
        [
            ("wq", wq_any, wq_ref),
            ("wk", wk_any, wk_ref),
            ("wv", wv_any, wv_ref),
            ("wo", wo_any, wo_ref),
            ("seg", seg_any, seg_ref),
            ("tok", tok_any, tok_t),
            ("gain", gain_any, gain_ref),
            ("wg", wg_any, wg_ref),
            ("steer", steer_any, steer_ref),
            ("sidx", sidx_any, sidx_ref),
            ("go", go_any, go_t),
        ]
    ):
        loads[name] = pltpu.make_async_copy(src, dst, loadsem.at[i])
        loads[name].start()

    barrier = pltpu.get_barrier_semaphore()
    for target in [cw, ccw, sib, after, before] + pairs:
        pl.semaphore_signal(barrier, inc=1, device_id=(target, h), device_id_type=MESH)
    for peer in peers:
        pl.semaphore_signal(barrier, inc=1, device_id=(me, peer), device_id_type=MESH)

    qbuf[me] = jnp.zeros(qbuf.shape[1:], BF16)
    obuf[me] = jnp.zeros(obuf.shape[1:], BF16)
    kv_t[...] = jnp.zeros(kv_t.shape, F32)
    for name in ("wq", "wk", "wv", "wo", "seg"):
        loads[name].wait()
    qbuf[me, :rows, :group_cols] = wq_ref[...]
    kv_t[:hd, :rows] = wk_ref[...].astype(F32)
    kv_t[hd:, :rows] = wv_ref[...].astype(F32)
    qbuf[me, :rows, group_cols:] = kv_t[...].T[:rows].astype(BF16)
    obuf[me, :rows, :] = wo_ref[...]
    segbuf[1] = jnp.broadcast_to(seg_ref[...], segbuf.shape[1:])

    pl.semaphore_wait(barrier, 5 + steps + H - 1)

    def remote(src, dst, send, recv, seq, head):
        return pltpu.make_async_remote_copy(
            src_ref=src,
            dst_ref=dst,
            send_sem=send,
            recv_sem=recv,
            device_id=(seq, head),
            device_id_type=MESH,
        )

    targets = (cw, ccw, sib)
    piece = qbuf.shape[1] // PIECES

    def q_copy(slot, way, i):
        part = pl.ds(i * piece, piece)
        return remote(
            qbuf.at[slot, part],
            qbuf.at[slot, part],
            qsend.at[way, slot, i],
            qrecv.at[slot, i],
            targets[way],
            h,
        )

    def o_copy(slot, way, i):
        part = pl.ds(i * piece, piece)
        return remote(
            obuf.at[slot, part],
            obuf.at[slot, part],
            osend.at[way, slot, i],
            orecv.at[slot, i],
            targets[way],
            h,
        )

    every = range(PIECES)
    for i in every:
        for way in range(3):
            q_copy(me, way, i).start()
    seg_copy = remote(segbuf.at[1], segbuf.at[0], segsem.at[0], segsem.at[1], after, h)
    seg_copy.start()

    def q_fwd(t):
        a, b = at(pos + C - t), at(pos + t)
        for i in every:
            q_copy(a, 0, i).wait_recv()
            q_copy(a, 0, i).start()
            q_copy(a, 2, i).start()
            q_copy(b, 1, i).wait_recv()

            @pl.when(t < half - 1)
            def _():
                q_copy(b, 1, i).start()

            q_copy(b, 2, i).start()

    def o_fwd(t):
        b, a = at(pos + t), at(pos + C - t)
        for i in every:
            o_copy(b, 1, i).wait_recv()
            o_copy(b, 1, i).start()
            o_copy(b, 2, i).start()
            o_copy(a, 0, i).wait_recv()

            @pl.when(t < half - 1)
            def _():
                o_copy(a, 0, i).start()

            o_copy(a, 2, i).start()

    same = lax.broadcasted_iota(jnp.int32, (T, T), 0) == lax.broadcasted_iota(jnp.int32, (T, T), 1)

    def column(row):
        return jnp.sum(
            jnp.where(same, jnp.broadcast_to(row, (T, T)), 0), axis=1, keepdims=True
        )

    for name in ("gain", "wg", "steer", "sidx"):
        loads[name].wait()
    vec_t[0:1] = gain_ref[...].reshape(1, D)
    vec_t[1:2] = wg_ref[...].reshape(1, D)
    vec_p[...] = jnp.zeros(vec_p.shape, F32)
    steer_p[...] = jnp.zeros(steer_p.shape, BF16)
    for c in range(S // 2):
        cols = slice(c * 2 * rows, (c + 1) * 2 * rows)
        vec_p[c, :, : 2 * rows] = vec_t[:, cols]
        steer_p[c, :, : 2 * rows] = steer_ref[:, cols]
    gap = jnp.zeros((T, norm_c.shape[2] - rows), F32)

    def halves(value):
        low = jnp.concatenate([value[:, :rows], gap], axis=1)
        high = jnp.concatenate([value[:, rows : 2 * rows], gap], axis=1)
        return low.astype(BF16), high.astype(BF16)

    def pair_rows(value, c):
        fill = jnp.zeros((tok_p.shape[2] - 2 * rows, T), F32)
        return jnp.concatenate([value[c * 2 * rows : (c + 1) * 2 * rows], fill], axis=0).T

    loads["tok"].wait()
    tokens = tok_t[...].astype(F32)
    inverse = column(
        lax.rsqrt(jnp.sum(tokens * tokens, axis=0, keepdims=True) * (1.0 / D) + EPSILON)
    )
    gate_sum = jnp.zeros(tok_p.shape[1:], F32)
    for c in range(S // 2):
        part = pair_rows(tokens, c)
        tok_p[c] = part.astype(BF16)
        normed = (part * inverse * vec_p[c, 0:1]).astype(BF16).astype(F32)
        norm_c[2 * c], norm_c[2 * c + 1] = halves(normed)
        gate_sum = gate_sum + normed * vec_p[c, 1:2]
    gate = jax.nn.sigmoid(jnp.sum(gate_sum, axis=1, keepdims=True))

    def q_acc(slot):
        qacc[...] += dot(norm_c[slot], qbuf[slot])

    def q_sib(slot):
        for i in every:
            q_copy(slot, 2, i).wait_recv()
        q_acc(slot)

    def q_work(t):
        a, b = at(pos + C - t), at(pos + t)
        q_acc(a)
        q_acc(b)
        q_sib(a + other)
        q_sib(b + other)

    q_fwd(1)
    for i in every:
        for way in range(3):
            o_copy(me, way, i).start()
    qacc[...] = dot(norm_c[me], qbuf[me])
    q_sib(sib)
    loads["go"].wait()
    grads = go_t[...].astype(F32)
    for c in range(S // 2):
        part = pair_rows(grads, c)
        go_p[c] = part.astype(BF16)
        go_c[2 * c], go_c[2 * c + 1] = halves(part)

    def q_both(t, carry):
        q_fwd(t)
        q_work(t - 1)
        return carry

    lax.fori_loop(2, half, q_both, 0)
    q_work(half - 1)
    far = at(pos + half)
    for i in every:
        q_copy(far, 0, i).wait_recv()
        q_copy(far, 2, i).start()
    q_acc(far)
    q_sib(far + other)

    qkv = qacc[...].astype(BF16)
    kvall[T:] = qkv[:, group_cols:]
    kv_copy = remote(
        kvall.at[pl.ds(T, T)], kvall.at[pl.ds(0, T)], kvsem.at[0], kvsem.at[1], after, h
    )
    kv_copy.start()

    sidx_row = sidx_ref[...]
    sidx_col = column(sidx_row)
    one_hot_b = (
        (lax.broadcasted_iota(jnp.int32, (T, steer_count), 1) == sidx_col).astype(F32).astype(BF16)
    )
    one_hot_t = (lax.broadcasted_iota(jnp.int32, (steer_count, T), 0) == sidx_row).astype(F32)

    def logit_step(c, total):
        return total + go_p[c].astype(F32) * dot(one_hot_b, steer_p[c])

    logit_sum = lax.fori_loop(0, S // 2, logit_step, jnp.zeros(go_p.shape[1:], F32))
    grad_logit = gate * (1.0 - gate) * jnp.sum(logit_sum, axis=1, keepdims=True)

    @pl.loop(0, share)
    def _(j):
        sacc[0, j] = jnp.dot(
            one_hot_t,
            gate * go_p[h * share + j].astype(F32),
            precision=HIGHEST,
            preferred_element_type=F32,
        )

    def s_copy(k):
        return remote(sacc.at[k], srecv.at[k], ssend.at[k], srsem.at[k], pairs[k], h)

    def s_finish(k):
        s_copy(k).wait_recv()
        sacc[k + 1] = sacc[k] + srecv[k]

    s_copy(0).start()

    def gate_step(c, total):
        return total + vec_p[c, 1:2] * vec_p[c, 0:1] * tok_p[c].astype(F32)

    gate_terms = lax.fori_loop(0, S // 2, gate_step, jnp.zeros(go_p.shape[1:], F32))
    row_gate = grad_logit * inverse * jnp.sum(gate_terms, axis=1, keepdims=True)

    seg_copy.wait_recv()
    halo_seg = jnp.where(me > 0, segbuf[0, 0:1, :], -1)
    seg_row = seg_ref[...]
    query_seg = column(seg_row)
    key_seg = jnp.concatenate([halo_seg, seg_row], axis=1)
    distance = (
        lax.broadcasted_iota(jnp.int32, (T, 2 * T), 0)
        - lax.broadcasted_iota(jnp.int32, (T, 2 * T), 1)
        + T
    )
    mask = (distance >= 0) & (distance < WIN) & (query_seg == key_seg)

    kv_copy.wait_recv()
    keys = kvall[:, :hd]
    values = kvall[:, hd:]
    mixed_parts = []
    for i in range(heads):
        scores = dot_t(qkv[:, i * hd : (i + 1) * hd], keys) * scale
        scores = jnp.where(mask, scores, -1e30)
        raised = jnp.exp(scores - jnp.max(scores, axis=1, keepdims=True))
        probs = raised / jnp.sum(raised, axis=1, keepdims=True)
        pbuf[i] = probs
        mixed_parts.append(dot(probs.astype(BF16), values).astype(BF16))
        if i == heads // 2 - 1:
            o_fwd(1)
        if i == heads - 1:
            o_fwd(2)
    mixed_t = jnp.concatenate(mixed_parts, axis=1).astype(F32).T.astype(BF16)

    def joined(low, high):
        fill = jnp.zeros((abuf.shape[2] - 2 * rows, T), F32)
        return jnp.concatenate([low[:rows], high[:rows], fill], axis=0).T.astype(BF16)

    def a_copy(pair):
        return remote(
            abuf.at[pair],
            arecv.at[h, pair % share],
            asend.at[pair],
            arsem.at[h, pair % share],
            me,
            pair // share,
        )

    def o_acc(slot):
        for i in every:
            o_copy(slot + other, 2, i).wait_recv()
        pair = slot // 2
        low, high = obuf[2 * pair], obuf[2 * pair + 1]
        abuf[pair] = joined(dot(low, mixed_t), dot(high, mixed_t))

        @pl.when(pair // share != h)
        def _():
            a_copy(pair).start()

        gmacc[...] += dot(go_c[2 * pair], low) + dot(go_c[2 * pair + 1], high)

    def o_work(t):
        o_acc(at(pos + t))
        o_acc(at(pos + C - t))

    gmacc[...] = jnp.zeros(gmacc.shape, F32)
    o_acc(me)
    o_work(1)

    def o_both(t, carry):
        o_fwd(t)
        o_work(t - 1)
        return carry

    lax.fori_loop(3, half, o_both, 0)
    for i in every:
        o_copy(far, 1, i).wait_recv()
        o_copy(far, 2, i).start()
    s_finish(0)
    s_copy(1).start()
    o_work(half - 1)
    o_acc(far)

    grad_mixed = gmacc[...].astype(BF16)
    grad_query = []
    grad_keys = jnp.zeros((2 * T, hd), F32)
    grad_values = jnp.zeros((2 * T, hd), F32)
    for i in range(heads):
        part = grad_mixed[:, i * hd : (i + 1) * hd]
        probs = pbuf[i]
        grad_prob = dot_t(part, values)
        delta = jnp.sum(probs * grad_prob, axis=1, keepdims=True)
        grad_scores = (probs * (grad_prob - delta) * scale).astype(BF16)
        grad_query.append(dot(grad_scores, keys).astype(BF16))
        grad_keys = grad_keys + t_dot(grad_scores, qkv[:, i * hd : (i + 1) * hd])
        grad_values = grad_values + t_dot(probs.astype(BF16), part)
    grad_kv = jnp.concatenate([grad_keys, grad_values], axis=1)
    hgsend[...] = grad_kv[:T].astype(BF16)
    hg_copy = remote(hgsend, hgrecv, hgsem.at[0], hgsem.at[1], before, h)
    hg_copy.start()
    s_finish(1)
    s_copy(2).start()

    for j in range(share):
        c = h * share + j
        total = abuf[c].astype(F32)
        for peer in peers:
            remote(
                abuf.at[c], arecv.at[peer, j], asend.at[c], arsem.at[peer, j], me, peer
            ).wait_recv()
            total = total + arecv[peer, j].astype(F32)
        steer_rows = dot(one_hot_b, steer_p[c])
        out = tok_p[c].astype(F32) + total + gate * steer_rows
        out_t[j * 2 * rows : (j + 1) * 2 * rows] = out.T[: 2 * rows]
    lay_ref[...] = out_t[...].astype(BF16)

    s_finish(2)
    s_copy(3).start()
    hg_copy.wait_recv()
    kv_back = (grad_kv[T:] + hgrecv[...].astype(F32)).astype(BF16)
    grad_t = jnp.concatenate(grad_query + [kv_back], axis=1).astype(F32).T.astype(BF16)

    def g_copy(pair):
        return remote(
            gbuf.at[pair],
            grecv.at[h, pair % share],
            gsend.at[pair],
            grsem.at[h, pair % share],
            me,
            pair // share,
        )

    def g_step(i, total):
        c = ((h + 1) * share + i) % (S // 2)
        term = joined(dot(qbuf[2 * c], grad_t), dot(qbuf[2 * c + 1], grad_t))
        gbuf[c] = term

        @pl.when(c // share != h)
        def _():
            g_copy(c).start()

        return total + term.astype(F32) * vec_p[c, 0:1] * tok_p[c].astype(F32)

    row_terms = lax.fori_loop(0, S // 2, g_step, jnp.zeros(go_p.shape[1:], F32))
    row_own = jnp.sum(row_terms, axis=1, keepdims=True) * inverse
    as_row = jnp.sum(jnp.where(same, jnp.broadcast_to(row_own, (T, T)), 0.0), axis=0, keepdims=True)
    rbuf[...] = jnp.broadcast_to(as_row, rbuf.shape)

    def r_copy(d):
        return remote(rbuf, rrecv.at[h], rsend.at[d], rrsem.at[h], me, peers[d])

    for d in range(H - 1):
        r_copy(d).start()
    for k in range(3, steps):
        s_finish(k)
        if k + 1 < steps:
            s_copy(k + 1).start()

    row_total = row_own + row_gate
    for j in range(share):
        sgrad_ref[:, j * 2 * rows : (j + 1) * 2 * rows] = sacc[steps, j][:, : 2 * rows]
    for peer in peers:
        remote(rbuf, rrecv.at[peer], rsend.at[0], rrsem.at[peer], me, peer).wait_recv()
        row_total = row_total + column(rrecv[peer, 0:1, :])
    row_mean = row_total * (1.0 / D)

    for j in range(share):
        c = h * share + j
        total = gbuf[c].astype(F32)
        for peer in peers:
            remote(
                gbuf.at[c], grecv.at[peer, j], gsend.at[c], grsem.at[peer, j], me, peer
            ).wait_recv()
            total = total + grecv[peer, j].astype(F32)
        scaled = (total + grad_logit * vec_p[c, 1:2]) * vec_p[c, 0:1]
        unit = tok_p[c].astype(F32) * inverse
        out = go_p[c].astype(F32) + inverse * (scaled - unit * row_mean)
        out_t[j * 2 * rows : (j + 1) * 2 * rows] = out.T[: 2 * rows]
    gtok_ref[...] = out_t[...].astype(BF16)

    seg_copy.wait_send()
    kv_copy.wait_send()
    hg_copy.wait_send()
    for k in range(steps):
        s_copy(k).wait_send()
    for d in range(H - 1):
        r_copy(d).wait_send()

    def sent(i, carry):
        c = ((h + 1) * share + i) % (S // 2)
        a_copy(c).wait_send()
        g_copy(c).wait_send()
        return carry

    lax.fori_loop(0, S // 2 - share, sent, 0)
    for i in every:
        for way in range(3):
            q_copy(me, way, i).wait_send()
            o_copy(me, way, i).wait_send()

    def ring_sent(t, carry):
        a, b = at(pos + C - t), at(pos + t)
        for i in every:
            q_copy(a, 0, i).wait_send()
            o_copy(b, 1, i).wait_send()

            @pl.when(t < half - 1)
            def _():
                q_copy(b, 1, i).wait_send()
                o_copy(a, 0, i).wait_send()

            for slot in (a, b):
                q_copy(slot, 2, i).wait_send()
                o_copy(slot, 2, i).wait_send()
        return carry

    lax.fori_loop(1, half, ring_sent, 0)
    for i in every:
        q_copy(far, 2, i).wait_send()
        o_copy(far, 2, i).wait_send()


def shards(
    S,
    H,
    tokens,
    gain,
    w_query,
    w_key,
    w_value,
    w_out,
    w_gate,
    steering,
    segment_ids,
    steer_index,
    grad_out,
):
    T, D = tokens.shape
    rows, group_cols = w_query.shape
    hd = w_key.shape[1]
    heads = group_cols // hd
    wide = group_cols + 2 * hd
    pad = -(-rows // (16 * PIECES)) * 16 * PIECES
    pairs = S // H // 2
    pair_wide = -(-2 * rows // 128) * 128
    steps = S.bit_length() - 1
    steer_count = steering.shape[0]
    dma = pltpu.SemaphoreType.DMA
    vmem = pltpu.VMEM
    scratch = [
        vmem((S, pad, wide), BF16),
        vmem((S, pad, group_cols), BF16),
        vmem((D, T), BF16),
        vmem((D,), F32),
        vmem((D,), F32),
        vmem((rows, group_cols), BF16),
        vmem((hd, rows), BF16),
        vmem((hd, rows), BF16),
        vmem((rows, group_cols), BF16),
        vmem((steer_count, D), BF16),
        vmem((1, T), jnp.int32),
        vmem((1, T), jnp.int32),
        vmem((D, T), BF16),
        vmem((2 * hd, -(-rows // 128) * 128), F32),
        vmem((2, D), F32),
        vmem((S // 2, T, pair_wide), BF16),
        vmem((S // 2, T, pair_wide), BF16),
        vmem((S, T, pad), BF16),
        vmem((S, T, pad), BF16),
        vmem((S // 2, 2, pair_wide), F32),
        vmem((S // 2, steer_count, pair_wide), BF16),
        vmem((T, wide), F32),
        vmem((T, group_cols), F32),
        vmem((2 * T, 2 * hd), BF16),
        vmem((2, 8, T), jnp.int32),
        vmem((heads, T, 2 * T), F32),
        vmem((S // 2, T, pair_wide), BF16),
        vmem((H, pairs, T, pair_wide), BF16),
        vmem((S // 2, T, pair_wide), BF16),
        vmem((H, pairs, T, pair_wide), BF16),
        vmem((8, T), F32),
        vmem((H, 8, T), F32),
        vmem((T, 2 * hd), BF16),
        vmem((T, 2 * hd), BF16),
        vmem((steps + 1, pairs, steer_count, pair_wide), F32),
        vmem((steps, pairs, steer_count, pair_wide), F32),
        dma((3, S, PIECES)),
        dma((S, PIECES)),
        dma((3, S, PIECES)),
        dma((S, PIECES)),
        dma((2,)),
        dma((2,)),
        dma((2,)),
        dma((S // 2,)),
        dma((H, pairs)),
        dma((S // 2,)),
        dma((H, pairs)),
        dma((max(H - 1, 1),)),
        dma((H,)),
        dma((steps,)),
        dma((steps,)),
        dma((11,)),
        vmem((D // H, T), F32),
    ]
    far_off = pl.BlockSpec(memory_space=pl.ANY)
    layer_t, grad_t, steer_grad = pl.pallas_call(
        functools.partial(kernel, S, H),
        out_shape=(
            jax.ShapeDtypeStruct((D // H, T), BF16),
            jax.ShapeDtypeStruct((D // H, T), BF16),
            jax.ShapeDtypeStruct((steer_count, D // H), F32),
        ),
        in_specs=[far_off] * 11,
        out_specs=[pl.BlockSpec(memory_space=pltpu.VMEM)] * 3,
        scratch_shapes=scratch,
        compiler_params=pltpu.CompilerParams(
            collective_id=0, has_side_effects=True, vmem_limit_bytes=60 * 1024 * 1024
        ),
    )(
        tokens.T,
        gain,
        w_gate,
        w_query,
        w_key.T,
        w_value.T,
        w_out,
        steering,
        segment_ids.reshape(1, T),
        steer_index.reshape(1, T),
        grad_out.T,
    )
    return layer_t.T, grad_t.T, steer_grad


def solution(mesh):
    placed = (
        P("seq", None),
        P(),
        P("seq", "head"),
        P("seq", "head"),
        P("seq", "head"),
        P("seq", "head"),
        P(),
        P(),
        P("seq"),
        P("seq"),
        P("seq", None),
    )
    return jax.shard_map(
        functools.partial(shards, mesh.shape["seq"], mesh.shape["head"]),
        mesh=mesh,
        in_specs=placed,
        out_specs=(P("seq", "head"), P("seq", "head"), P(None, "head")),
        check_vma=False,
    )
```
